32 devices in a mesh: group: 2 (over x), ha: 16 (over z, y, core).
Axes of the slice: x: 2, y: 2, z: 4, core: 2. Of those that a mesh axis runs over, the one named last changes fastest.
Arguments:
- volume: bfloat16 [64, 64, 16, 128], P(('group', 'ha')), parts along dimension 0, may hold values from -6 to 6
- skip_grad: bfloat16 [64, 64, 16, 128], P(('group', 'ha')), parts along dimension 0, may hold values from -6 to 6
- coarse_grad: bfloat16 [32, 8, 64, 128], P(('group', 'ha')), parts along dimension 0, may hold values from -6 to 6
- w_first: bfloat16 [3, 3, 3, 64, 64], replicated, may hold values from -0.15625 to 0.15625
- w_second: bfloat16 [3, 3, 3, 64, 64], replicated, may hold values from -0.15625 to 0.15625
- w_down: bfloat16 [2, 2, 2, 64, 128], replicated, may hold values from -0.25 to 0.25
- w_coarse: bfloat16 [3, 3, 3, 128, 128], replicated, may hold values from -0.109375 to 0.109375
Outputs:
- input_grad: float32 [64, 64, 16, 128], P(('group', 'ha')), parts along dimension 0
- first_kernel: float32 [6, 3, 3, 64, 64], P('group'), parts along dimension 0
- second_kernel: float32 [6, 3, 3, 64, 64], P('group'), parts along dimension 0
- down_kernel: float32 [4, 2, 2, 64, 128], P('group'), parts along dimension 0
- coarse_kernel: float32 [6, 3, 3, 128, 128], P('group'), parts along dimension 0
The draws below stay inside these ranges and needn't reach their ends.
There are 2 independent parts, one for each index of `group`. The reference program is written for one: setup_inputs(seed, part) draws one part's arguments, and reference() takes and returns one part's arrays. A program takes and returns all parts, laid end to end along the dimension named above; an argument that names none is the same for every part. Nothing has to cross between parts.
All inputs are finite; a program needn't handle non-finite values.
Results may differ from the reference program's by a relative error of at most 0.017.
Values may be sent and summed in bfloat16 or wider, within the bound.
No kernel may reach another device: no remote copies, remote signals or barrier semaphores. Data moves between devices by JAX's collectives and lax.ppermute only.
A program may use at most 128 MiB of HBM per device.

```python
import jax
import jax.numpy as jnp
from jax import lax

C1 = 64
C2 = 128
W = 16
DP = 128
NH = 32


def shard_levels(stream_key, extent, cuts, least, largest):
    def one(axis_at, blocks):
        steps = jax.random.uniform(jax.random.fold_in(jax.random.fold_in(stream_key, 6), axis_at), (blocks,), jnp.float32, least / len(cuts), largest / len(cuts))
        return jnp.repeat(jnp.exp(steps), extent[axis_at] // blocks).reshape((-1,) + (1,) * (len(extent) - axis_at - 1))

    level = one(*cuts[0])
    for cut in cuts[1:]:
        level = level * one(*cut)
    return level


def bell_draw(key, dims, scale, limit, split=(), dtype=jnp.bfloat16):
    drawn = scale * jax.random.normal(key, dims, jnp.float32)
    if split:
        drawn = drawn * shard_levels(key, dims, split, -0.22, 0.18)
    return jnp.clip(drawn, -limit, limit).astype(dtype)


def setup_inputs(seed: int = 0, part: int = 0) -> dict:
    arg_keys = jax.random.split(jax.random.key(seed), 8)
    part_splits = jax.random.split(jax.random.fold_in(arg_keys[7], part), 8)
    return {
        "volume": bell_draw(part_splits[0], (NH, C1, W, DP), 1.0, 6.0, ((0, 16),)),
        "skip_grad": bell_draw(part_splits[1], (NH, C1, W, DP), 1.0, 6.0, ((0, 16),)),
        "coarse_grad": bell_draw(part_splits[2], (NH // 2, W // 2, DP // 2, C2), 1.0, 6.0, ((0, 16),)),
        "w_first": bell_draw(arg_keys[3], (3, 3, 3, C1, C1), (27 * C1) ** -0.5, 0.15625),
        "w_second": bell_draw(arg_keys[4], (3, 3, 3, C1, C1), (27 * C1) ** -0.5, 0.15625),
        "w_down": bell_draw(arg_keys[5], (2, 2, 2, C1, C2), (8 * C1) ** -0.5, 0.25),
        "w_coarse": bell_draw(arg_keys[6], (3, 3, 3, C2, C2), (27 * C2) ** -0.5, 0.109375),
    }


FINE = ('NHCWD', 'HWDIO', 'NHCWD')
FINE_BACK = ('NHCWD', 'HWDOI', 'NHCWD')
FINE_WGRAD = ('CHNWD', 'IHOWD', 'HWDNC')
COARSE = ('NHWDC', 'HWDIO', 'NHWDC')
COARSE_BACK = ('NHWDC', 'HWDOI', 'NHWDC')
COARSE_WGRAD = ('CHWDN', 'IHWDO', 'HWDNC')

def stencil(source, kernel, numbers):
    return lax.conv_general_dilated(source[None], kernel, (1, 1, 1), ((1, 1), (1, 1), (1, 1)), dimension_numbers=numbers, preferred_element_type=jnp.float32)[0]

def kernel_grad(source, cotangent, numbers):
    return lax.conv_general_dilated(source[None], cotangent[None], (1, 1, 1), ((1, 1), (1, 1), (1, 1)), dimension_numbers=numbers, preferred_element_type=jnp.float32)

def silu_slope(value):
    sigma = jax.nn.sigmoid(value)
    return sigma * (1.0 + value * (1.0 - sigma))

def down_forward(source, kernel):
    num_rows, num_chan, num_cols, num_deep = source.shape
    blocks = source.reshape(num_rows // 2, 2, num_chan, num_cols // 2, 2, num_deep // 2, 2)
    return jnp.einsum('haiwbdc,abcio->hwdo', blocks.astype(jnp.float32), kernel.astype(jnp.float32))

def down_back(cotangent, kernel):
    spread = jnp.einsum('hwdo,abcio->haiwbdc', cotangent.astype(jnp.float32), kernel.astype(jnp.float32))
    shape_in = spread.shape
    return spread.reshape(shape_in[0] * 2, shape_in[2], shape_in[3] * 2, shape_in[5] * 2)

def down_weight(source, cotangent):
    num_rows, num_chan, num_cols, num_deep = source.shape
    blocks = source.reshape(num_rows // 2, 2, num_chan, num_cols // 2, 2, num_deep // 2, 2)
    return jnp.einsum('haiwbdc,hwdo->abcio', blocks.astype(jnp.float32), cotangent.astype(jnp.float32))

def reference(volume, skip_grad, coarse_grad, w_first, w_second, w_down, w_coarse):
    first_pre = stencil(volume, w_first, FINE)
    first_act = jax.nn.silu(first_pre).astype(jnp.bfloat16)
    second_pre = stencil(first_act, w_second, FINE)
    second_act = jax.nn.silu(second_pre).astype(jnp.bfloat16)
    pooled = down_forward(second_act, w_down).astype(jnp.bfloat16)
    coarse_pre = stencil(pooled, w_coarse, COARSE)
    coarse_delta = (coarse_grad.astype(jnp.float32) * silu_slope(coarse_pre)).astype(jnp.bfloat16)
    coarse_kernel = kernel_grad(pooled, coarse_delta, COARSE_WGRAD)
    pooled_grad = stencil(coarse_delta, w_coarse[::-1, ::-1, ::-1], COARSE_BACK).astype(jnp.bfloat16)
    down_kernel = down_weight(second_act, pooled_grad)
    second_delta = ((down_back(pooled_grad, w_down) + skip_grad.astype(jnp.float32)) * silu_slope(second_pre)).astype(jnp.bfloat16)
    second_kernel = kernel_grad(first_act, second_delta, FINE_WGRAD)
    first_delta = (stencil(second_delta, w_second[::-1, ::-1, ::-1], FINE_BACK) * silu_slope(first_pre)).astype(jnp.bfloat16)
    first_kernel = kernel_grad(volume, first_delta, FINE_WGRAD)
    input_grad = stencil(first_delta, w_first[::-1, ::-1, ::-1], FINE_BACK)
    return (input_grad, first_kernel, second_kernel, down_kernel, coarse_kernel)
```

```python
import functools

import jax
import jax.numpy as jnp
from jax import lax
from jax.experimental import pallas as pl
from jax.experimental.pallas import tpu as pltpu
from jax.sharding import PartitionSpec as P

BF = jnp.bfloat16
F32 = jnp.float32
NT = (((1,), (1,)), ((), ()))
TN = (((0,), (0,)), ((), ()))
AXIS = "ha"


def dot(a, b, dims=(((1,), (0,)), ((), ()))):
    return lax.dot_general(a, b, dims, preferred_element_type=F32)


def call(body, outs, *args, scratch=(), flops=10**9, smem=0):
    in_specs = [pl.BlockSpec(memory_space=pltpu.SMEM)] * smem
    in_specs += [pl.BlockSpec(memory_space=pltpu.VMEM)] * (len(args) - smem)
    size = sum(a.size * a.dtype.itemsize for a in args)
    return pl.pallas_call(
        body,
        out_shape=[jax.ShapeDtypeStruct(s, d) for s, d in outs],
        in_specs=in_specs,
        out_specs=[pl.BlockSpec(memory_space=pltpu.VMEM)] * len(outs),
        scratch_shapes=list(scratch),
        compiler_params=pltpu.CompilerParams(vmem_limit_bytes=48 * 2**20),
        cost_estimate=pl.CostEstimate(flops=flops, bytes_accessed=size, transcendentals=0),
    )(*args)


def neighbours(array):
    size = lax.axis_size(AXIS)
    up = [(i, i + 1) for i in range(size - 1)]
    down = [(j, i) for i, j in up]
    return up, down


def from_before(array):
    return lax.ppermute(array, AXIS, neighbours(array)[0])


def from_after(array):
    return lax.ppermute(array, AXIS, neighbours(array)[1])


def sigmoid(value):
    return 1.0 / (1.0 + jnp.exp(-value))


def fine_pair(rows, w_ref, col):
    num = rows[0].shape[0]
    chan, deep = rows[0].shape[1], rows[0].shape[2]
    none = jnp.zeros((chan, deep), BF)
    sides = []
    for at in (col, col + 1):
        tiles = []
        for row in rows:
            for k in (-1, 0, 1):
                tiles.append(row[at + k] if 0 <= at + k < num else none)
        sides.append(jnp.concatenate(tiles, 0))
    y = dot(w_ref[...], jnp.concatenate(sides, 1))
    lane = lax.broadcasted_iota(jnp.int32, (chan, deep), 1)
    outs = []
    for side in range(2):
        part = y[:, side * deep : (side + 1) * deep]
        left = jnp.where(lane == 0, 0.0, pltpu.roll(part[:chan], 1, 1))
        right = jnp.where(lane == deep - 1, 0.0, pltpu.roll(part[2 * chan :], deep - 1, 1))
        outs.append(part[chan : 2 * chan] + left + right)
    return outs


def fine_grad(sources, deltas, a_scr, b_scr, out_ref):
    num, chan, deep = deltas[0].shape
    lane = lax.broadcasted_iota(jnp.int32, (chan, deep), 1)
    for r in range(2):
        for at in range(num):
            cols = slice((r * num + at) * deep, (r * num + at + 1) * deep)
            for kh in range(3):
                for kw in range(3):
                    tap = kh * 3 + kw
                    src = at + kw - 1
                    tile = sources[r + kh][src] if 0 <= src < num else jnp.zeros((chan, deep), BF)
                    a_scr[tap * chan : (tap + 1) * chan, cols] = tile
            value = deltas[r][at]
            wide = value.astype(F32)
            b_scr[:chan, cols] = jnp.where(
                lane == deep - 1, 0.0, pltpu.roll(wide, deep - 1, 1)
            ).astype(BF)
            b_scr[chan : 2 * chan, cols] = value
            b_scr[2 * chan :, cols] = jnp.where(lane == 0, 0.0, pltpu.roll(wide, 1, 1)).astype(BF)
    acc = dot(a_scr[...], b_scr[...], NT).astype(BF)
    for tap in range(9):
        rows = slice(tap * chan, (tap + 1) * chan)
        out_ref[rows, :] = acc[rows, : 2 * chan]
    for tap in range(0, 10, 2):
        first = acc[tap * chan : (tap + 1) * chan, 2 * chan :]
        if tap + 1 < 9:
            other = acc[(tap + 1) * chan : (tap + 2) * chan, 2 * chan :]
        else:
            other = jnp.zeros_like(first)
        at = (9 + tap // 2) * chan
        out_ref[at : at + chan, :] = jnp.concatenate([first, other], 1)


def fine_grad_scratch(num, chan, deep):
    return (
        pltpu.VMEM((9 * chan, 2 * num * deep), BF),
        pltpu.VMEM((3 * chan, 2 * num * deep), BF),
    )


def coarse_stack(rows, deep):
    size, chan = rows[0].shape
    none = jnp.zeros((deep, chan), BF)
    tiles = []
    for row in rows:
        value = row[...]
        tiles.append(jnp.concatenate([none, value[: size - deep]], 0))
        tiles.append(value)
        tiles.append(jnp.concatenate([value[deep:], none], 0))
    return jnp.concatenate(tiles, 1)


def coarse_conv(rows, w_ref, deep):
    size, chan = rows[0].shape
    y = dot(coarse_stack(rows, deep), w_ref[...])
    at = lax.rem(lax.broadcasted_iota(jnp.int32, (size, chan), 0), deep)
    left = jnp.where(at == 0, 0.0, pltpu.roll(y[:, :chan], 1, 0))
    right = jnp.where(at == deep - 1, 0.0, pltpu.roll(y[:, 2 * chan :], size - 1, 0))
    return y[:, chan : 2 * chan] + left + right


def forward_kernel(
    flags, before, own, after, w_first, w_second, w_down, perm,
    v0, v1, v2, v3, f0, f1, f2, f3, slope1, slope2, act_t, pooled,
    first_scr, rows_scr,
):
    num = f0.shape[0]
    deep = f0.shape[2]
    volumes = [v0, v1, v2, v3]
    firsts = [f0, f1, f2, f3]
    sources = [(before, 0), (before, 1), (own, 0), (own, 1), (after, 0), (after, 1)]
    for i, (ref, r) in enumerate(sources):
        turned = pltpu.einshape("cwd->wcd", ref[r])
        rows_scr[i] = turned
        if 1 <= i <= 4:
            volumes[i - 1][...] = turned
    for r in range(4):
        rows = [rows_scr.at[r + k] for k in range(3)]
        for col in range(0, num, 2):
            for side, pre in enumerate(fine_pair(rows, w_first, col)):
                sigma = sigmoid(pre)
                act = pre * sigma
                if r == 0:
                    act = jnp.where(flags[0] > 0, act, 0.0)
                if r == 3:
                    act = jnp.where(flags[1] > 0, act, 0.0)
                firsts[r][col + side] = act.astype(BF)
                if 1 <= r <= 2:
                    slope1[r - 1, col + side] = sigma * (1.0 + pre * (1.0 - sigma))
    half = deep // 2
    for r in range(2):
        rows = firsts[r : r + 3]
        for col in range(0, num, 2):
            acts = []
            for side, pre in enumerate(fine_pair(rows, w_second, col)):
                sigma = sigmoid(pre)
                acts.append((pre * sigma).astype(BF))
                slope2[r, col + side] = sigma * (1.0 + pre * (1.0 - sigma))
            both = jnp.concatenate(acts, 0)
            wide = both.shape[0]
            turned = dot(perm[...], both, NT).astype(BF)
            at = slice(col // 2 * half, (col // 2 + 1) * half)
            for c in range(2):
                lanes = slice((2 * r + c) * wide, (2 * r + c + 1) * wide)
                act_t[at, lanes] = turned[c * half : (c + 1) * half]
    pooled[...] = dot(act_t[...], w_down[...]).astype(BF)


def coarse_kernel_body(deep, before, own, after, grad, w, delta):
    pre = coarse_conv([before, own, after], w, deep)
    sigma = sigmoid(pre)
    slope = sigma * (1.0 + pre * (1.0 - sigma))
    delta[...] = (grad[...].astype(F32) * slope).astype(BF)


def coarse_grad_body(deep, before, own, after, delta, out):
    size, chan = own.shape
    wide = delta[...].astype(F32)
    at = lax.rem(lax.broadcasted_iota(jnp.int32, (size, chan), 0), deep)
    up = jnp.where(at == deep - 1, 0.0, pltpu.roll(wide, size - 1, 0)).astype(BF)
    down = jnp.where(at == 0, 0.0, pltpu.roll(wide, 1, 0)).astype(BF)
    shifted = jnp.concatenate([up, delta[...], down], 1)
    stack = coarse_stack([before, own, after], deep)
    acc = dot(stack, shifted, TN).astype(BF)
    rows = acc.shape[0]
    for k in range(3):
        out[k * rows : (k + 1) * rows, :] = acc[:, k * chan : (k + 1) * chan]


def second_delta_body(deep, before, own, after, w, w_up, spread, skip, slope, pg, d0, d1):
    value = coarse_conv([before, own, after], w, deep).astype(BF)
    pg[...] = value
    turned = value.T
    chan = turned.shape[0]
    half = d0.shape[1]
    fine = d0.shape[2]
    outs = [d0, d1]
    for m in range(turned.shape[1] // (2 * deep)):
        up = dot(turned[:, 2 * m * deep : 2 * (m + 1) * deep], spread[...]).astype(BF)
        parts = [
            jnp.concatenate([up[:, (2 * s + c) * fine : (2 * s + c + 1) * fine] for s in range(2)], 1)
            for c in range(2)
        ]
        back = dot(w_up[...], jnp.concatenate(parts, 0))
        for s in range(2):
            for a in range(2):
                for b in range(2):
                    rows = slice((2 * a + b) * half, (2 * a + b + 1) * half)
                    at = 4 * m + 2 * s + b
                    total = back[rows, s * fine : (s + 1) * fine] + skip[a, at].astype(F32)
                    outs[a][at] = (total * slope[a, at]).astype(BF)


def second_grad_body(s0, s1, s2, s3, d0, d1, act_t, pg, out, down, a_scr, b_scr):
    fine_grad([s0, s1, s2, s3], [d0, d1], a_scr, b_scr, out)
    down[...] = dot(act_t[...], pg[...], TN).astype(BF)


def first_delta_body(r0, r1, r2, r3, w, slope, d0, d1):
    rows = [r0, r1, r2, r3]
    outs = [d0, d1]
    for r in range(2):
        for col in range(0, d0.shape[0], 2):
            for side, value in enumerate(fine_pair(rows[r : r + 3], w, col)):
                outs[r][col + side] = (value * slope[r, col + side]).astype(BF)


def first_grad_body(s0, s1, s2, s3, d0, d1, out, a_scr, b_scr):
    fine_grad([s0, s1, s2, s3], [d0, d1], a_scr, b_scr, out)


def input_grad_body(r0, r1, r2, r3, w, out, scr):
    rows = [r0, r1, r2, r3]
    for r in range(2):
        for col in range(0, r0.shape[0], 2):
            for side, value in enumerate(fine_pair(rows[r : r + 3], w, col)):
                scr[col + side] = value
        out[r] = pltpu.einshape("wcd->cwd", scr[...])


def reduced(array):
    size = lax.axis_size(AXIS)
    me = lax.axis_index(AXIS)
    steps = []
    step = 1
    while step < size:
        steps.append(step)
        step *= 2
    for step in steps:
        half = array.shape[0] // 2
        bit = (me // step) % 2
        mine = lax.dynamic_slice_in_dim(array, bit * half, half, 0)
        other = lax.dynamic_slice_in_dim(array, (1 - bit) * half, half, 0)
        got = lax.ppermute(other, AXIS, [(i, i ^ step) for i in range(size)])
        array = (mine.astype(F32) + got.astype(F32)).astype(BF)
    for step in steps[::-1]:
        bit = (me // step) % 2
        got = lax.ppermute(array, AXIS, [(i, i ^ step) for i in range(size)])
        low = jnp.where(bit == 0, array, got)
        high = jnp.where(bit == 0, got, array)
        array = jnp.concatenate([low, high], 0)
    return array


def fine_unpack(flat, chan):
    pairs = flat[: 9 * chan].reshape(9, chan, 2, chan)
    last = flat[9 * chan :].reshape(5, chan, 2, chan).transpose(0, 2, 1, 3).reshape(10, chan, chan)[:9]
    stacked = jnp.stack([pairs[:, :, 0], pairs[:, :, 1], last], 1)
    return stacked.reshape(3, 3, 3, chan, chan).astype(F32)


def body(volume, skip_grad, coarse_grad, w_first, w_second, w_down, w_coarse):
    _, chan, num, deep = volume.shape
    wide = w_coarse.shape[-1]
    half = deep // 2
    size = num // 2 * half
    index = lax.axis_index(AXIS)
    flags = jnp.stack([index, lax.axis_size(AXIS) - 1 - index]).astype(jnp.int32)

    before, after = from_before(volume), from_after(volume)

    forward = lambda w: w.transpose(2, 4, 0, 1, 3).reshape(3 * chan, 9 * chan)
    backward = lambda w: w[::-1, ::-1, ::-1].transpose(2, 3, 0, 1, 4).reshape(3 * chan, 9 * chan)
    first_f, second_f = forward(w_first), forward(w_second)
    first_b, second_b = backward(w_first), backward(w_second)
    coarse_f = w_coarse.transpose(0, 1, 3, 2, 4).reshape(9 * wide, 3 * wide)
    coarse_b = w_coarse[::-1, ::-1, ::-1].transpose(0, 1, 4, 2, 3).reshape(9 * wide, 3 * wide)
    down_f = w_down.transpose(0, 2, 1, 3, 4).reshape(8 * chan, wide)
    down_b = w_down.transpose(0, 1, 3, 2, 4).reshape(4 * chan, 2 * wide)
    skip = skip_grad.transpose(0, 2, 1, 3)

    at = lax.broadcasted_iota(jnp.int32, (deep, deep), 1)
    q = lax.broadcasted_iota(jnp.int32, (deep, deep), 0)
    perm = (at == 2 * (q % half) + q // half).astype(BF)
    row = lax.broadcasted_iota(jnp.int32, (deep, 4 * deep), 0)
    lane = lax.broadcasted_iota(jnp.int32, (deep, 4 * deep), 1)
    spread = (
        (lane // (2 * deep) == row // half)
        & (lane % deep == 2 * (row % half) + (lane // deep) % 2)
    ).astype(BF)

    fine = ((num, chan, deep), BF)
    fine32 = ((2, num, chan, deep), F32)
    coarse = ((size, wide), BF)
    outs = call(
        forward_kernel,
        [fine] * 8 + [fine32] * 2 + [((size, 8 * chan), BF), coarse],
        flags, before, volume, after, first_f, second_f, down_f, perm,
        scratch=(pltpu.VMEM((8, 128), F32), pltpu.VMEM((6, num, chan, deep), BF)),
        smem=1,
    )
    volumes, firsts = outs[:4], outs[4:8]
    slope1, slope2, act_t, pooled = outs[8:]

    rows = [from_before(pooled), pooled, from_after(pooled)]
    (delta,) = call(
        functools.partial(coarse_kernel_body, half), [coarse],
        *rows, coarse_grad.reshape(size, wide), coarse_f,
    )
    delta_rows = [from_before(delta), delta, from_after(delta)]
    (coarse_sum,) = call(
        functools.partial(coarse_grad_body, half), [((27 * wide, wide), BF)], *rows, delta
    )
    pg, d0, d1 = call(
        functools.partial(second_delta_body, half), [coarse, fine, fine],
        *delta_rows, coarse_b, down_b, spread, skip, slope2,
    )
    packed = ((14 * chan, 2 * chan), BF)
    second_rows = [from_before(d1), d0, d1, from_after(d0)]
    second_sum, down_sum = call(
        second_grad_body, [packed, ((8 * chan, wide), BF)], *firsts, d0, d1, act_t, pg,
        scratch=fine_grad_scratch(num, chan, deep),
    )
    e0, e1 = call(first_delta_body, [fine, fine], *second_rows, second_b, slope1)
    first_rows = [from_before(e1), e0, e1, from_after(e0)]
    (first_sum,) = call(
        first_grad_body, [packed], *volumes, e0, e1, scratch=fine_grad_scratch(num, chan, deep)
    )
    (input_grad,) = call(
        input_grad_body, [((2, chan, num, deep), F32)], *first_rows, first_b,
        scratch=(pltpu.VMEM((num, chan, deep), F32),),
    )

    coarse_sum = reduced(coarse_sum)
    middle = reduced(jnp.concatenate([second_sum, down_sum], 0))
    first_sum = reduced(first_sum)
    split = second_sum.shape[0]
    return (
        input_grad,
        fine_unpack(first_sum, chan),
        fine_unpack(middle[:split], chan),
        middle[split:].reshape(2, 2, 2, chan, wide).transpose(0, 2, 1, 3, 4).astype(F32),
        coarse_sum.reshape(3, 3, 3, wide, wide).transpose(1, 2, 0, 3, 4).astype(F32),
    )


def solution(mesh):
    rows = P(("group", "ha"), None, None, None)
    kernels = P("group", None, None, None, None)
    return jax.shard_map(
        body,
        mesh=mesh,
        in_specs=(rows, rows, rows, P(), P(), P(), P()),
        out_specs=(rows, kernels, kernels, kernels, kernels),
        check_vma=False,
    )
```

```python
import functools

import jax
import jax.numpy as jnp
from jax import lax
from jax.experimental import pallas as pl
from jax.experimental.pallas import tpu as pltpu
from jax.sharding import PartitionSpec as P

BF = jnp.bfloat16
F32 = jnp.float32
NT = (((1,), (1,)), ((), ()))
TN = (((0,), (0,)), ((), ()))
AXIS = "ha"


def dot(a, b, dims=(((1,), (0,)), ((), ()))):
    return lax.dot_general(a, b, dims, preferred_element_type=F32)


def call(body, outs, *args, scratch=(), flops=10**9, smem=0):
    in_specs = [pl.BlockSpec(memory_space=pltpu.SMEM)] * smem
    in_specs += [pl.BlockSpec(memory_space=pltpu.VMEM)] * (len(args) - smem)
    size = sum(a.size * a.dtype.itemsize for a in args)
    return pl.pallas_call(
        body,
        out_shape=[jax.ShapeDtypeStruct(s, d) for s, d in outs],
        in_specs=in_specs,
        out_specs=[pl.BlockSpec(memory_space=pltpu.VMEM)] * len(outs),
        scratch_shapes=list(scratch),
        compiler_params=pltpu.CompilerParams(vmem_limit_bytes=48 * 2**20),
        cost_estimate=pl.CostEstimate(flops=flops, bytes_accessed=size, transcendentals=0),
    )(*args)


def neighbours(array):
    size = lax.axis_size(AXIS)
    up = [(i, i + 1) for i in range(size - 1)]
    down = [(j, i) for i, j in up]
    return up, down


def from_before(array):
    return lax.ppermute(array, AXIS, neighbours(array)[0])


def from_after(array):
    return lax.ppermute(array, AXIS, neighbours(array)[1])


def swapped(array, stride):
    size = lax.axis_size(AXIS)
    return lax.ppermute(array, AXIS, [(i, i ^ stride) for i in range(size)])


def shifted(array, stride, by):
    size = lax.axis_size(AXIS)
    return lax.ppermute(array, AXIS, [(i, (i + by * stride) % size) for i in range(size)])


def sigmoid(value):
    return 0.5 + 0.5 * jnp.tanh(0.5 * value)


def fine_pair(rows, w_ref, col):
    num = rows[0].shape[0]
    chan, deep = rows[0].shape[1], rows[0].shape[2]
    none = jnp.zeros((chan, deep), BF)
    sides = []
    for at in (col, col + 1):
        tiles = []
        for row in rows:
            for k in (-1, 0, 1):
                tiles.append(row[at + k] if 0 <= at + k < num else none)
        sides.append(jnp.concatenate(tiles, 0))
    y = dot(w_ref[...], jnp.concatenate(sides, 1))
    lane = lax.broadcasted_iota(jnp.int32, (chan, deep), 1)
    outs = []
    for side in range(2):
        part = y[:, side * deep : (side + 1) * deep]
        left = jnp.where(lane == 0, 0.0, pltpu.roll(part[:chan], 1, 1))
        right = jnp.where(lane == deep - 1, 0.0, pltpu.roll(part[2 * chan :], deep - 1, 1))
        outs.append(part[chan : 2 * chan] + left + right)
    return outs


def put(halves, block, value):
    num = value.shape[0]
    each = halves.shape[1] // num
    at = block % each * num
    halves[block // each, at : at + num, :] = value


def deal(halves, bit, mine, other):
    mine[...] = halves[bit]
    other[...] = halves[1 - bit]


def fine_grad(sources, deltas, a_scr, b_scr, halves):
    num, chan, deep = deltas[0].shape
    lane = lax.broadcasted_iota(jnp.int32, (chan, deep), 1)
    for r in range(2):
        for at in range(num):
            cols = slice((r * num + at) * deep, (r * num + at + 1) * deep)
            for kh in range(3):
                for kw in range(3):
                    tap = kh * 3 + kw
                    src = at + kw - 1
                    tile = sources[r + kh][src] if 0 <= src < num else jnp.zeros((chan, deep), BF)
                    a_scr[tap * chan : (tap + 1) * chan, cols] = tile
            value = deltas[r][at]
            wide = value.astype(F32)
            b_scr[:chan, cols] = jnp.where(
                lane == deep - 1, 0.0, pltpu.roll(wide, deep - 1, 1)
            ).astype(BF)
            b_scr[chan : 2 * chan, cols] = value
            b_scr[2 * chan :, cols] = jnp.where(lane == 0, 0.0, pltpu.roll(wide, 1, 1)).astype(BF)
    acc = dot(a_scr[...], b_scr[...], NT).astype(BF)
    for tap in range(9):
        put(halves, tap, acc[tap * chan : (tap + 1) * chan, : 2 * chan])
    for tap in range(0, 10, 2):
        first = acc[tap * chan : (tap + 1) * chan, 2 * chan :]
        if tap + 1 < 9:
            other = acc[(tap + 1) * chan : (tap + 2) * chan, 2 * chan :]
        else:
            other = jnp.zeros_like(first)
        put(halves, 9 + tap // 2, jnp.concatenate([first, other], 1))


def fine_grad_scratch(num, chan, deep):
    return (
        pltpu.VMEM((9 * chan, 2 * num * deep), BF),
        pltpu.VMEM((3 * chan, 2 * num * deep), BF),
    )


def coarse_stack(rows, deep):
    size, chan = rows[0].shape
    none = jnp.zeros((deep, chan), BF)
    tiles = []
    for row in rows:
        value = row[...]
        tiles.append(jnp.concatenate([none, value[: size - deep]], 0))
        tiles.append(value)
        tiles.append(jnp.concatenate([value[deep:], none], 0))
    return jnp.concatenate(tiles, 1)


def coarse_conv(rows, w_ref, deep, *dims):
    size, chan = rows[0].shape
    y = dot(coarse_stack(rows, deep), w_ref[...], *dims)
    at = lax.rem(lax.broadcasted_iota(jnp.int32, (size, chan), 0), deep)
    left = jnp.where(at == 0, 0.0, pltpu.roll(y[:, :chan], 1, 0))
    right = jnp.where(at == deep - 1, 0.0, pltpu.roll(y[:, 2 * chan :], size - 1, 0))
    return y[:, chan : 2 * chan] + left + right


def prepare_kernel(
    volume, skip, w_first, w_second, w_down, w_coarse,
    v0, v1, skip_t, first_f, second_f, first_b, second_b, coarse_f, coarse_b, down_f, down_b,
):
    chan = w_first.shape[1]
    wide = w_coarse.shape[1]
    eye = (
        lax.broadcasted_iota(jnp.int32, (chan, chan), 0)
        == lax.broadcasted_iota(jnp.int32, (chan, chan), 1)
    ).astype(BF)
    for w, ahead, back in ((w_first, first_f, first_b), (w_second, second_f, second_b)):
        for kd in range(3):
            stack = jnp.concatenate([w[3 * j + kd] for j in range(9)], 0)
            ahead[kd * chan : (kd + 1) * chan, :] = dot(eye, stack, NT).astype(BF)
            back[kd * chan : (kd + 1) * chan, :] = jnp.concatenate(
                [w[26 - 3 * j - kd] for j in range(9)], 1
            )
    for j in range(9):
        for kd in range(3):
            rows = slice(j * wide, (j + 1) * wide)
            cols = slice(kd * wide, (kd + 1) * wide)
            coarse_f[rows, cols] = w_coarse[3 * j + kd]
            coarse_b[cols, rows] = w_coarse[26 - 3 * j - kd]
    for a in range(2):
        for b in range(2):
            for c in range(2):
                value = w_down[4 * a + 2 * b + c]
                at = 4 * a + 2 * c + b
                down_f[at * chan : (at + 1) * chan, :] = value
                at = 2 * a + b
                down_b[at * chan : (at + 1) * chan, c * wide : (c + 1) * wide] = value
    for r, out in enumerate((v0, v1)):
        out[...] = pltpu.einshape("cwd->wcd", volume[r])
        skip_t[r] = pltpu.einshape("cwd->wcd", skip[r])


def forward_kernel(
    flags, before, own0, own1, after, w_first, w_second, w_down,
    v0, v3, f0, f1, f2, f3, slope1, slope2, act_t, pooled, rows_scr,
):
    num, chan, deep = own0.shape
    half = deep // 2
    firsts = [f0, f1, f2, f3]
    rows_scr[0] = pltpu.einshape("cwd->wcd", before[0])
    v0[...] = pltpu.einshape("cwd->wcd", before[1])
    v3[...] = pltpu.einshape("cwd->wcd", after[0])
    rows_scr[1] = pltpu.einshape("cwd->wcd", after[1])
    sources = [rows_scr.at[0], v0, own0, own1, v3, rows_scr.at[1]]
    for r in range(4):
        for col in range(0, num, 2):
            for side, pre in enumerate(fine_pair(sources[r : r + 3], w_first, col)):
                sigma = sigmoid(pre)
                act = pre * sigma
                slope = sigma + act * (1.0 - sigma)
                if r == 0:
                    act = jnp.where(flags[0] > 0, act, 0.0)
                    slope = jnp.where(flags[0] > 0, slope, 0.0)
                if r == 3:
                    act = jnp.where(flags[1] > 0, act, 0.0)
                    slope = jnp.where(flags[1] > 0, slope, 0.0)
                firsts[r][col + side] = act.astype(BF)
                slope1[r, col + side] = slope
    at = lax.broadcasted_iota(jnp.int32, (deep, deep), 1)
    q = lax.broadcasted_iota(jnp.int32, (deep, deep), 0)
    perm = (at == 2 * lax.rem(q, half) + (q >= half).astype(jnp.int32)).astype(BF)
    for r in range(2):
        rows = firsts[r : r + 3]
        for col in range(0, num, 2):
            acts = []
            for side, pre in enumerate(fine_pair(rows, w_second, col)):
                sigma = sigmoid(pre)
                act = pre * sigma
                acts.append(act.astype(BF))
                slope2[r, col + side] = sigma + act * (1.0 - sigma)
            both = jnp.concatenate(acts, 0)
            wide = both.shape[0]
            turned = dot(perm, both, NT).astype(BF)
            at = slice(col // 2 * half, (col // 2 + 1) * half)
            for c in range(2):
                lanes = slice((2 * r + c) * wide, (2 * r + c + 1) * wide)
                act_t[at, lanes] = turned[c * half : (c + 1) * half]
    pooled[...] = dot(act_t[...], w_down[...]).astype(BF)


def coarse_delta_body(deep, before, own, after, grad, w, delta):
    pre = coarse_conv([before, own, after], w, deep)
    sigma = sigmoid(pre)
    slope = sigma + pre * sigma * (1.0 - sigma)
    delta[...] = (grad[...].astype(F32) * slope).astype(BF)


def coarse_grad_body(deep, flags, before, own, after, delta, mine, other, halves):
    size, chan = own.shape
    wide = delta[...].astype(F32)
    at = lax.rem(lax.broadcasted_iota(jnp.int32, (size, chan), 0), deep)
    up = jnp.where(at == deep - 1, 0.0, pltpu.roll(wide, size - 1, 0)).astype(BF)
    down = jnp.where(at == 0, 0.0, pltpu.roll(wide, 1, 0)).astype(BF)
    moved = jnp.concatenate([up, delta[...], down], 1)
    stack = coarse_stack([before, own, after], deep)
    acc = dot(stack, moved, TN).astype(BF)
    piece = chan // 2
    for k in range(3):
        for j in range(18):
            value = acc[j * piece : (j + 1) * piece, k * chan : (k + 1) * chan]
            put(halves, 18 * k + j, value)
    deal(halves, flags[2], mine, other)


def second_delta_body(deep, before, own, after, w, w_up, skip, slope, pg, delta):
    value = coarse_conv([before, own, after], w, deep, NT).astype(BF)
    pg[...] = value
    turned = value.T
    half = delta.shape[2]
    fine = delta.shape[3]
    row = lax.broadcasted_iota(jnp.int32, (fine, 4 * fine), 0)
    lane = lax.broadcasted_iota(jnp.int32, (fine, 4 * fine), 1)
    odd = (lax.rem(lane, 2 * fine) >= fine).astype(jnp.int32)
    same = (lane >= 2 * fine) == (row >= deep)
    spread = (same & (lax.rem(lane, fine) == 2 * lax.rem(row, deep) + odd)).astype(BF)
    for m in range(turned.shape[1] // (2 * deep)):
        up = dot(turned[:, 2 * m * deep : 2 * (m + 1) * deep], spread).astype(BF)
        parts = [
            jnp.concatenate([up[:, (2 * s + c) * fine : (2 * s + c + 1) * fine] for s in range(2)], 1)
            for c in range(2)
        ]
        back = dot(w_up[...], jnp.concatenate(parts, 0))
        for s in range(2):
            for a in range(2):
                for b in range(2):
                    rows = slice((2 * a + b) * half, (2 * a + b + 1) * half)
                    at = 4 * m + 2 * s + b
                    total = back[rows, s * fine : (s + 1) * fine] + skip[a, at].astype(F32)
                    delta[a, at] = (total * slope[a, at]).astype(BF)


def second_grad_body(flags, s0, s1, s2, s3, delta, act_t, pg, mine, other, a_scr, b_scr, halves):
    fine_grad([s0, s1, s2, s3], [delta.at[0], delta.at[1]], a_scr, b_scr, halves)
    down = dot(act_t[...], pg[...], TN).astype(BF)
    chan = s0.shape[1]
    for j in range(8):
        put(halves, 14 + j, down[j * chan : (j + 1) * chan])
    deal(halves, flags[2], mine, other)


def first_delta_body(
    flags, before, own, after, w, slope, s0, s1, s2, s3, delta, mine, other, a_scr, b_scr, halves
):
    rows = [ref.at[r] for ref in (before, own, after) for r in range(2)]
    for r in range(4):
        for col in range(0, delta.shape[1], 2):
            for side, value in enumerate(fine_pair(rows[r : r + 3], w, col)):
                delta[r, col + side] = (value * slope[r, col + side]).astype(BF)
    fine_grad([s0, s1, s2, s3], [delta.at[1], delta.at[2]], a_scr, b_scr, halves)
    deal(halves, flags[2], mine, other)


def input_grad_body(delta, w, out, scr):
    rows = [delta.at[r] for r in range(4)]
    for r in range(2):
        for col in range(0, delta.shape[1], 2):
            for side, value in enumerate(fine_pair(rows[r : r + 3], w, col)):
                scr[col + side] = value
        out[r] = pltpu.einshape("wcd->cwd", scr[...])


def added(*refs):
    values = [ref[...].astype(F32) for ref in refs]
    while len(values) > 1:
        half = len(values) // 2
        values = [values[t] + values[t + half] for t in range(half)]
    return values[0]


def split_body(flags, mine, got, keep, send):
    half = keep.shape[0]
    bit = flags[3]
    for side in range(2):
        rows = slice(side * half, (side + 1) * half)
        total = (mine[rows, :].astype(F32) + got[rows, :].astype(F32)).astype(BF)

        @pl.when(bit == side)
        def _():
            keep[...] = total

        @pl.when(bit != side)
        def _():
            send[...] = total


def add_body(*refs):
    refs[-1][...] = added(*refs[:-1]).astype(BF)


def order_body(flags, mine, got, out):
    bit = flags[3]
    out[bit] = mine[...]
    out[1 - bit] = got[...]


def block_of(halves, block, num):
    each = halves.shape[1] // num
    at = block % each * num
    return halves[block // each, at : at + num, :].astype(F32)


def fine_blocks(halves, out):
    chan = out.shape[1]
    for tap in range(9):
        value = block_of(halves, tap, chan)
        out[3 * tap] = value[:, :chan]
        out[3 * tap + 1] = value[:, chan:]
        value = block_of(halves, 9 + tap // 2, chan)
        out[3 * tap + 2] = value[:, chan:] if tap % 2 else value[:, :chan]


def gather_halves(flags, mine, got, halves):
    bit = flags[2]
    halves[bit] = mine[...].reshape(halves.shape[1:])
    halves[1 - bit] = got[...].reshape(halves.shape[1:])


def fine_unpack(flags, mine, got, out, halves):
    gather_halves(flags, mine, got, halves)
    fine_blocks(halves, out)


def middle_unpack(flags, mine, got, out, down, halves):
    gather_halves(flags, mine, got, halves)
    fine_blocks(halves, out)
    chan = out.shape[1]
    for a in range(2):
        for b in range(2):
            for c in range(2):
                down[4 * a + 2 * b + c] = block_of(halves, 14 + 4 * a + 2 * c + b, chan)


def coarse_unpack(flags, mine, got, out, halves):
    gather_halves(flags, mine, got, halves)
    piece = out.shape[1] // 2
    for k in range(3):
        for j in range(9):
            for s in range(2):
                out[3 * j + k, s * piece : (s + 1) * piece, :] = block_of(
                    halves, 18 * k + 2 * j + s, piece
                )


def reduced(flags, mine, other, unpack, outs):
    rows, lanes = mine.shape
    quarter = ((rows // 2, lanes), BF)
    got = swapped(other, 1)
    keep, send = call(split_body, [quarter] * 2, flags, mine, got, smem=1)
    (part,) = call(add_body, [quarter], keep, swapped(send, 2))
    parts = [part] + [shifted(part, 4, t) for t in range(1, lax.axis_size(AXIS) // 4)]
    (part,) = call(add_body, [quarter], *parts)
    (pair,) = call(
        order_body, [((2, rows // 2, lanes), BF)], flags, part, swapped(part, 2), smem=1
    )
    return call(
        unpack, outs, flags, pair, swapped(pair, 1), smem=1,
        scratch=(pltpu.VMEM((2, rows, lanes), BF),),
    )


def body(volume, skip_grad, coarse_grad, w_first, w_second, w_down, w_coarse):
    _, chan, num, deep = volume.shape
    wide = w_coarse.shape[-1]
    half = deep // 2
    size = num // 2 * half
    index = lax.axis_index(AXIS)
    flags = jnp.stack(
        [index, lax.axis_size(AXIS) - 1 - index, index % 2, (index // 2) % 2]
    ).astype(jnp.int32)

    fine = ((num, chan, deep), BF)
    coarse = ((size, wide), BF)
    two = ((2, num, chan, deep), BF)
    four = ((4, num, chan, deep), BF)

    before, after = from_before(volume), from_after(volume)
    v1, v2, skip, first_f, second_f, first_b, second_b, coarse_f, coarse_b, down_f, down_b = call(
        prepare_kernel,
        [fine, fine, two]
        + [((3 * chan, 9 * chan), BF)] * 4
        + [((9 * wide, 3 * wide), BF), ((3 * wide, 9 * wide), BF)]
        + [((8 * chan, wide), BF), ((4 * chan, 2 * wide), BF)],
        volume, skip_grad,
        w_first.reshape(27, chan, chan), w_second.reshape(27, chan, chan),
        w_down.reshape(8, chan, wide), w_coarse.reshape(27, wide, wide),
    )
    v0, v3, f0, f1, f2, f3, slope1, slope2, act_t, pooled = call(
        forward_kernel,
        [fine] * 6 + [(four[0], F32), (two[0], F32), ((size, 8 * chan), BF), coarse],
        flags, before, v1, v2, after, first_f, second_f, down_f,
        scratch=(pltpu.VMEM(*two),),
        smem=1,
    )
    rows = [from_before(pooled), pooled, from_after(pooled)]
    (delta,) = call(
        functools.partial(coarse_delta_body, half), [coarse],
        *rows, coarse_grad.reshape(size, wide), coarse_f,
    )
    delta_rows = [from_before(delta), delta, from_after(delta)]

    def dealt(blocks):
        return ((blocks // 2 * chan, 2 * chan), BF)

    def halves(blocks):
        return pltpu.VMEM((2, blocks // 2 * chan, 2 * chan), BF)

    coarse_sum = call(
        functools.partial(coarse_grad_body, half), [dealt(54)] * 2, flags, *rows, delta,
        scratch=(halves(54),), smem=1,
    )
    pg, second = call(
        functools.partial(second_delta_body, half), [coarse, two],
        *delta_rows, coarse_b, down_b, skip, slope2,
    )
    second_before, second_after = from_before(second), from_after(second)
    middle_sum = call(
        second_grad_body, [dealt(22)] * 2, flags, f0, f1, f2, f3, second, act_t, pg,
        scratch=fine_grad_scratch(num, chan, deep) + (halves(22),), smem=1,
    )
    first, *first_sum = call(
        first_delta_body, [four] + [dealt(14)] * 2,
        flags, second_before, second, second_after, second_b, slope1, v0, v1, v2, v3,
        scratch=fine_grad_scratch(num, chan, deep) + (halves(14),), smem=1,
    )
    (input_grad,) = call(
        input_grad_body, [((2, chan, num, deep), F32)], first, first_b,
        scratch=(pltpu.VMEM((num, chan, deep), F32),),
    )
    fine_out = ((27, chan, chan), F32)
    (coarse_out,) = reduced(flags, *coarse_sum, coarse_unpack, [((27, wide, wide), F32)])
    second_out, down_out = reduced(
        flags, *middle_sum, middle_unpack, [fine_out, ((8, chan, wide), F32)]
    )
    (first_out,) = reduced(flags, *first_sum, fine_unpack, [fine_out])
    return (
        input_grad,
        first_out.reshape(3, 3, 3, chan, chan),
        second_out.reshape(3, 3, 3, chan, chan),
        down_out.reshape(2, 2, 2, chan, wide),
        coarse_out.reshape(3, 3, 3, wide, wide),
    )


def solution(mesh):
    rows = P(("group", "ha"), None, None, None)
    kernels = P("group", None, None, None, None)
    return jax.shard_map(
        body,
        mesh=mesh,
        in_specs=(rows, rows, rows, P(), P(), P(), P()),
        out_specs=(rows, kernels, kernels, kernels, kernels),
        check_vma=False,
    )
```

```python
import functools

import jax
import jax.numpy as jnp
from jax import lax
from jax.experimental import pallas as pl
from jax.experimental.pallas import tpu as pltpu
from jax.sharding import PartitionSpec as P

BF = jnp.bfloat16
F32 = jnp.float32
NT = (((1,), (1,)), ((), ()))
TN = (((0,), (0,)), ((), ()))
AXIS = "ha"
COST = 10**9


def dot(a, b, dims=(((1,), (0,)), ((), ()))):
    return lax.dot_general(a, b, dims, preferred_element_type=F32)


def call(body, outs, *args, scratch=(), smem=0):
    in_specs = [pl.BlockSpec(memory_space=pltpu.SMEM)] * smem
    in_specs += [pl.BlockSpec(memory_space=pltpu.VMEM)] * (len(args) - smem)
    return pl.pallas_call(
        body,
        out_shape=[jax.ShapeDtypeStruct(s, d) for s, d in outs],
        in_specs=in_specs,
        out_specs=[pl.BlockSpec(memory_space=pltpu.VMEM)] * len(outs),
        scratch_shapes=list(scratch),
        compiler_params=pltpu.CompilerParams(vmem_limit_bytes=48 * 2**20),
        cost_estimate=pl.CostEstimate(flops=COST, bytes_accessed=2**20, transcendentals=0),
    )(*args)


def neighbours(array):
    size = lax.axis_size(AXIS)
    up = [(i, i + 1) for i in range(size - 1)]
    down = [(j, i) for i, j in up]
    return up, down


def from_before(array):
    return lax.ppermute(array, AXIS, neighbours(array)[0])


def from_after(array):
    return lax.ppermute(array, AXIS, neighbours(array)[1])


def swapped(array, stride):
    size = lax.axis_size(AXIS)
    return lax.ppermute(array, AXIS, [(i, i ^ stride) for i in range(size)])


def shifted(array, stride, by):
    size = lax.axis_size(AXIS)
    return lax.ppermute(array, AXIS, [(i, (i + by * stride) % size) for i in range(size)])


def sigmoid(value):
    return 0.5 + 0.5 * jnp.tanh(0.5 * value)


def fine_pair(rows, w_ref, col):
    num = rows[0].shape[0]
    chan, deep = rows[0].shape[1], rows[0].shape[2]
    none = jnp.zeros((chan, deep), BF)
    sides = []
    for at in (col, col + 1):
        tiles = []
        for row in rows:
            for k in (-1, 0, 1):
                tiles.append(row[at + k] if 0 <= at + k < num else none)
        sides.append(jnp.concatenate(tiles, 0))
    y = dot(w_ref[...], jnp.concatenate(sides, 1))
    lane = lax.broadcasted_iota(jnp.int32, (chan, deep), 1)
    outs = []
    for side in range(2):
        part = y[:, side * deep : (side + 1) * deep]
        left = jnp.where(lane == 0, 0.0, pltpu.roll(part[:chan], 1, 1))
        right = jnp.where(lane == deep - 1, 0.0, pltpu.roll(part[2 * chan :], deep - 1, 1))
        outs.append(part[chan : 2 * chan] + left + right)
    return outs


def put(halves, block, value):
    num = value.shape[0]
    each = halves.shape[1] // num
    at = block % each * num
    halves[block // each, at : at + num, :] = value


def deal(halves, bit, mine, other):
    mine[...] = halves[bit]
    other[...] = halves[1 - bit]


def fine_grad(sources, deltas, a_scr, b_scr, halves):
    num, chan, deep = deltas[0].shape
    lane = lax.broadcasted_iota(jnp.int32, (chan, deep), 1)
    for r in range(2):
        for at in range(num):
            cols = slice((r * num + at) * deep, (r * num + at + 1) * deep)
            for kh in range(3):
                for kw in range(3):
                    tap = kh * 3 + kw
                    src = at + kw - 1
                    tile = sources[r + kh][src] if 0 <= src < num else jnp.zeros((chan, deep), BF)
                    a_scr[tap * chan : (tap + 1) * chan, cols] = tile
            value = deltas[r][at]
            wide = value.astype(F32)
            b_scr[:chan, cols] = jnp.where(
                lane == deep - 1, 0.0, pltpu.roll(wide, deep - 1, 1)
            ).astype(BF)
            b_scr[chan : 2 * chan, cols] = value
            b_scr[2 * chan :, cols] = jnp.where(lane == 0, 0.0, pltpu.roll(wide, 1, 1)).astype(BF)
    acc = dot(a_scr[...], b_scr[...], NT).astype(BF)
    for tap in range(9):
        put(halves, tap, acc[tap * chan : (tap + 1) * chan, : 2 * chan])
    for tap in range(0, 10, 2):
        first = acc[tap * chan : (tap + 1) * chan, 2 * chan :]
        if tap + 1 < 9:
            other = acc[(tap + 1) * chan : (tap + 2) * chan, 2 * chan :]
        else:
            other = jnp.zeros_like(first)
        put(halves, 9 + tap // 2, jnp.concatenate([first, other], 1))


def fine_grad_scratch(num, chan, deep):
    return (
        pltpu.VMEM((9 * chan, 2 * num * deep), BF),
        pltpu.VMEM((3 * chan, 2 * num * deep), BF),
    )


def coarse_stack(rows, deep):
    size, chan = rows[0].shape
    none = jnp.zeros((deep, chan), BF)
    tiles = []
    for row in rows:
        value = row[...]
        tiles.append(jnp.concatenate([none, value[: size - deep]], 0))
        tiles.append(value)
        tiles.append(jnp.concatenate([value[deep:], none], 0))
    return jnp.concatenate(tiles, 1)


def coarse_conv(rows, w_ref, deep, *dims):
    size, chan = rows[0].shape
    y = dot(coarse_stack(rows, deep), w_ref[...], *dims)
    at = lax.rem(lax.broadcasted_iota(jnp.int32, (size, chan), 0), deep)
    left = jnp.where(at == 0, 0.0, pltpu.roll(y[:, :chan], 1, 0))
    right = jnp.where(at == deep - 1, 0.0, pltpu.roll(y[:, 2 * chan :], size - 1, 0))
    return y[:, chan : 2 * chan] + left + right


def prepare_kernel(
    volume, skip, w_first, w_second, w_down, w_coarse,
    v0, v1, skip_t, first_f, second_f, first_b, second_b, coarse_f, coarse_b, down_f, down_b,
):
    chan = w_first.shape[1]
    wide = w_coarse.shape[1]
    eye = (
        lax.broadcasted_iota(jnp.int32, (chan, chan), 0)
        == lax.broadcasted_iota(jnp.int32, (chan, chan), 1)
    ).astype(BF)
    for w, ahead, back in ((w_first, first_f, first_b), (w_second, second_f, second_b)):
        for kd in range(3):
            stack = jnp.concatenate([w[3 * j + kd] for j in range(9)], 0)
            ahead[kd * chan : (kd + 1) * chan, :] = dot(eye, stack, NT).astype(BF)
            back[kd * chan : (kd + 1) * chan, :] = jnp.concatenate(
                [w[26 - 3 * j - kd] for j in range(9)], 1
            )
    for j in range(9):
        for kd in range(3):
            rows = slice(j * wide, (j + 1) * wide)
            cols = slice(kd * wide, (kd + 1) * wide)
            coarse_f[rows, cols] = w_coarse[3 * j + kd]
            coarse_b[cols, rows] = w_coarse[26 - 3 * j - kd]
    for a in range(2):
        for b in range(2):
            for c in range(2):
                value = w_down[4 * a + 2 * b + c]
                at = 4 * a + 2 * c + b
                down_f[at * chan : (at + 1) * chan, :] = value
                at = 2 * a + b
                down_b[at * chan : (at + 1) * chan, c * wide : (c + 1) * wide] = value
    for r, out in enumerate((v0, v1)):
        out[...] = pltpu.einshape("cwd->wcd", volume[r])
        skip_t[r] = pltpu.einshape("cwd->wcd", skip[r])


def forward_kernel(
    flags, before, own0, own1, after, w_first, w_second, w_down,
    v0, v3, f0, f1, f2, f3, slope1, slope2, act_t, pooled, rows_scr,
):
    num, chan, deep = own0.shape
    half = deep // 2
    firsts = [f0, f1, f2, f3]
    rows_scr[0] = pltpu.einshape("cwd->wcd", before[0])
    v0[...] = pltpu.einshape("cwd->wcd", before[1])
    v3[...] = pltpu.einshape("cwd->wcd", after[0])
    rows_scr[1] = pltpu.einshape("cwd->wcd", after[1])
    sources = [rows_scr.at[0], v0, own0, own1, v3, rows_scr.at[1]]
    for r in range(4):
        for col in range(0, num, 2):
            for side, pre in enumerate(fine_pair(sources[r : r + 3], w_first, col)):
                sigma = sigmoid(pre)
                act = pre * sigma
                slope = sigma + act * (1.0 - sigma)
                if r == 0:
                    act = jnp.where(flags[0] > 0, act, 0.0)
                    slope = jnp.where(flags[0] > 0, slope, 0.0)
                if r == 3:
                    act = jnp.where(flags[1] > 0, act, 0.0)
                    slope = jnp.where(flags[1] > 0, slope, 0.0)
                firsts[r][col + side] = act.astype(BF)
                slope1[r, col + side] = slope
    at = lax.broadcasted_iota(jnp.int32, (deep, deep), 1)
    q = lax.broadcasted_iota(jnp.int32, (deep, deep), 0)
    perm = (at == 2 * lax.rem(q, half) + (q >= half).astype(jnp.int32)).astype(BF)
    for r in range(2):
        rows = firsts[r : r + 3]
        for col in range(0, num, 2):
            acts = []
            for side, pre in enumerate(fine_pair(rows, w_second, col)):
                sigma = sigmoid(pre)
                act = pre * sigma
                acts.append(act.astype(BF))
                slope2[r, col + side] = sigma + act * (1.0 - sigma)
            both = jnp.concatenate(acts, 0)
            wide = both.shape[0]
            turned = dot(perm, both, NT).astype(BF)
            at = slice(col // 2 * half, (col // 2 + 1) * half)
            for c in range(2):
                lanes = slice((2 * r + c) * wide, (2 * r + c + 1) * wide)
                act_t[at, lanes] = turned[c * half : (c + 1) * half]
    pooled[...] = dot(act_t[...], w_down[...]).astype(BF)


def coarse_delta_body(deep, before, own, after, grad, w, delta):
    pre = coarse_conv([before, own, after], w, deep)
    sigma = sigmoid(pre)
    slope = sigma + pre * sigma * (1.0 - sigma)
    delta[...] = (grad[...].astype(F32) * slope).astype(BF)


def coarse_grad_body(deep, flags, before, own, after, delta, mine, other, halves):
    size, chan = own.shape
    wide = delta[...].astype(F32)
    at = lax.rem(lax.broadcasted_iota(jnp.int32, (size, chan), 0), deep)
    up = jnp.where(at == deep - 1, 0.0, pltpu.roll(wide, size - 1, 0)).astype(BF)
    down = jnp.where(at == 0, 0.0, pltpu.roll(wide, 1, 0)).astype(BF)
    moved = jnp.concatenate([up, delta[...], down], 1)
    stack = coarse_stack([before, own, after], deep)
    acc = dot(stack, moved, TN).astype(BF)
    piece = chan // 2
    for k in range(3):
        for j in range(18):
            value = acc[j * piece : (j + 1) * piece, k * chan : (k + 1) * chan]
            put(halves, 18 * k + j, value)
    for j in range(54, 2 * halves.shape[1] // piece):
        put(halves, j, jnp.zeros((piece, chan), BF))
    deal(halves, flags[2], mine, other)


def second_delta_body(deep, before, own, after, w, w_up, skip, slope, pg, delta):
    value = coarse_conv([before, own, after], w, deep, NT).astype(BF)
    pg[...] = value
    turned = value.T
    half = delta.shape[2]
    fine = delta.shape[3]
    row = lax.broadcasted_iota(jnp.int32, (fine, 4 * fine), 0)
    lane = lax.broadcasted_iota(jnp.int32, (fine, 4 * fine), 1)
    odd = (lax.rem(lane, 2 * fine) >= fine).astype(jnp.int32)
    same = (lane >= 2 * fine) == (row >= deep)
    spread = (same & (lax.rem(lane, fine) == 2 * lax.rem(row, deep) + odd)).astype(BF)
    for m in range(turned.shape[1] // (2 * deep)):
        up = dot(turned[:, 2 * m * deep : 2 * (m + 1) * deep], spread).astype(BF)
        parts = [
            jnp.concatenate([up[:, (2 * s + c) * fine : (2 * s + c + 1) * fine] for s in range(2)], 1)
            for c in range(2)
        ]
        back = dot(w_up[...], jnp.concatenate(parts, 0))
        for s in range(2):
            for a in range(2):
                for b in range(2):
                    rows = slice((2 * a + b) * half, (2 * a + b + 1) * half)
                    at = 4 * m + 2 * s + b
                    total = back[rows, s * fine : (s + 1) * fine] + skip[a, at].astype(F32)
                    delta[a, at] = (total * slope[a, at]).astype(BF)


def second_grad_body(flags, s0, s1, s2, s3, delta, act_t, pg, mine, other, a_scr, b_scr, halves):
    fine_grad([s0, s1, s2, s3], [delta.at[0], delta.at[1]], a_scr, b_scr, halves)
    down = dot(act_t[...], pg[...], TN).astype(BF)
    chan = s0.shape[1]
    for j in range(8):
        put(halves, 14 + j, down[j * chan : (j + 1) * chan])
    deal(halves, flags[2], mine, other)


def back_row(rows, w, slope, at, out):
    for col in range(0, out.shape[0], 2):
        for side, value in enumerate(fine_pair(rows, w, col)):
            out[col + side] = (value * slope[at, col + side]).astype(BF)


def first_delta_body(
    flags, before, own, after, w, slope, s0, s1, s2, s3, e1, e2, mine, other, a_scr, b_scr, halves
):
    rows = [before.at[1], own.at[0], own.at[1], after.at[0]]
    back_row(rows[:3], w, slope, 1, e1)
    back_row(rows[1:], w, slope, 2, e2)
    fine_grad([s0, s1, s2, s3], [e1, e2], a_scr, b_scr, halves)
    deal(halves, flags[2], mine, other)


def input_grad_body(before, own, after, w_second, slope, e1, e2, w, out, scr, e0, e3):
    back_row([before.at[0], before.at[1], own.at[0]], w_second, slope, 0, e0)
    back_row([own.at[1], after.at[0], after.at[1]], w_second, slope, 3, e3)
    rows = [e0, e1, e2, e3]
    for r in range(2):
        for col in range(0, e1.shape[0], 2):
            for side, value in enumerate(fine_pair(rows[r : r + 3], w, col)):
                scr[col + side] = value
        out[r] = pltpu.einshape("wcd->cwd", scr[...])


def added(*refs):
    values = [ref[...].astype(F32) for ref in refs]
    while len(values) > 1:
        half = len(values) // 2
        values = [values[t] + values[t + half] for t in range(half)]
    return values[0]


def split_body(count, flags, *refs):
    keep, send = refs[2 * count :]
    at = 0
    for mine, got in zip(refs[:count], refs[count : 2 * count]):
        half = mine.shape[0] // 2
        for side in range(2):
            rows = slice(side * half, (side + 1) * half)
            total = (mine[rows, :].astype(F32) + got[rows, :].astype(F32)).astype(BF)

            @pl.when(flags[3] == side)
            def _():
                keep[at : at + half, :] = total

            @pl.when(flags[3] != side)
            def _():
                send[at : at + half, :] = total

        at += half


def chunk_body(flags, keep, got, *refs):
    *outs, scr = refs
    num, rows, _ = scr.shape
    for i in range(num):
        at = slice(i * rows, (i + 1) * rows)
        scr[i] = (keep[at, :].astype(F32) + got[at, :].astype(F32)).astype(BF)
    for t, out in enumerate(outs):
        out[...] = scr[lax.rem(flags[4] + t, num)]


def gather_body(flags, *refs):
    *parts, out = refs
    num = out.shape[0]
    for t, part in enumerate(parts):
        out[lax.rem(flags[4] + num - t, num)] = part[...]


def add_body(*refs):
    refs[-1][...] = added(*refs[:-1]).astype(BF)


def order_body(flags, mine, got, out):
    bit = flags[3]
    out[bit] = mine[...].reshape(out.shape[1:])
    out[1 - bit] = got[...].reshape(out.shape[1:])


def block_of(halves, block, num):
    each = halves.shape[1] // num
    at = block % each * num
    return halves[block // each, at : at + num, :].astype(F32)


def fine_blocks(halves, out):
    chan = out.shape[1]
    for tap in range(9):
        value = block_of(halves, tap, chan)
        out[3 * tap] = value[:, :chan]
        out[3 * tap + 1] = value[:, chan:]
        value = block_of(halves, 9 + tap // 2, chan)
        out[3 * tap + 2] = value[:, chan:] if tap % 2 else value[:, :chan]


def gather_halves(flags, mine, got, *arrays):
    at = 0
    for halves in arrays:
        rows = halves.shape[1] // 2
        for side in range(2):
            to = slice(side * rows, (side + 1) * rows)
            halves[flags[2], to, :] = mine[side, at : at + rows, :]
            halves[1 - flags[2], to, :] = got[side, at : at + rows, :]
        at += rows


def fine_unpack(flags, mine, got, first, second, down, middle_halves, first_halves):
    gather_halves(flags, mine, got, middle_halves, first_halves)
    fine_blocks(first_halves, first)
    fine_blocks(middle_halves, second)
    chan = first.shape[1]
    for a in range(2):
        for b in range(2):
            for c in range(2):
                down[4 * a + 2 * b + c] = block_of(middle_halves, 14 + 4 * a + 2 * c + b, chan)


def coarse_unpack(flags, mine, got, out, halves):
    gather_halves(flags, mine, got, halves)
    piece = out.shape[1] // 2
    for k in range(3):
        for j in range(9):
            for s in range(2):
                out[3 * j + k, s * piece : (s + 1) * piece, :] = block_of(
                    halves, 18 * k + 2 * j + s, piece
                )


def tied(first, *others):
    return lax.optimization_barrier((first,) + others)[0]


def halved(flags, *pairs):
    mine, got = zip(*pairs)
    rows = sum(m.shape[0] for m in mine) // 2
    return call(
        functools.partial(split_body, len(pairs)), [((rows, mine[0].shape[1]), BF)] * 2,
        flags, *mine, *got, smem=1,
    )


def summed(*parts):
    return call(add_body, [(parts[0].shape, BF)], *parts)[0]


def chunks(flags, keep, got):
    num = lax.axis_size(AXIS) // 4
    shape = (keep.shape[0] // num, keep.shape[1])
    return call(
        chunk_body, [(shape, BF)] * num, flags, keep, got, smem=1,
        scratch=(pltpu.VMEM((num,) + shape, BF),),
    )


def sent(parts):
    return [shifted(part, 4, t) for t, part in enumerate(parts, 1)]


def gathered(flags, parts):
    return call(gather_body, [((len(parts),) + parts[0].shape, BF)], flags, *parts, smem=1)[0]


def paired(flags, part, got):
    lanes = part.shape[-1]
    return call(
        order_body, [((2, part.size // lanes, lanes), BF)], flags, part, got, smem=1
    )[0]


def body(volume, skip_grad, coarse_grad, w_first, w_second, w_down, w_coarse):
    _, chan, num, deep = volume.shape
    wide = w_coarse.shape[-1]
    half = deep // 2
    size = num // 2 * half
    index = lax.axis_index(AXIS)
    flags = jnp.stack(
        [index, lax.axis_size(AXIS) - 1 - index, index % 2, (index // 2) % 2, index // 4]
    ).astype(jnp.int32)

    fine = ((num, chan, deep), BF)
    coarse = ((size, wide), BF)
    two = ((2, num, chan, deep), BF)

    before, after = from_before(volume), from_after(volume)
    v1, v2, skip, first_f, second_f, first_b, second_b, coarse_f, coarse_b, down_f, down_b = call(
        prepare_kernel,
        [fine, fine, two]
        + [((3 * chan, 9 * chan), BF)] * 4
        + [((9 * wide, 3 * wide), BF), ((3 * wide, 9 * wide), BF)]
        + [((8 * chan, wide), BF), ((4 * chan, 2 * wide), BF)],
        volume, skip_grad,
        w_first.reshape(27, chan, chan), w_second.reshape(27, chan, chan),
        w_down.reshape(8, chan, wide), w_coarse.reshape(27, wide, wide),
    )
    v0, v3, f0, f1, f2, f3, slope1, slope2, act_t, pooled = call(
        forward_kernel,
        [fine] * 6 + [((4, num, chan, deep), F32), (two[0], F32), ((size, 8 * chan), BF), coarse],
        flags, before, v1, v2, after, first_f, second_f, down_f,
        scratch=(pltpu.VMEM(*two),),
        smem=1,
    )
    rows = [from_before(pooled), pooled, from_after(pooled)]
    (delta,) = call(
        functools.partial(coarse_delta_body, half), [coarse],
        *rows, coarse_grad.reshape(size, wide), coarse_f,
    )
    delta_rows = [from_before(delta), delta, from_after(delta)]

    def dealt(blocks):
        return ((blocks // 2 * chan, 2 * chan), BF)

    def halves(blocks):
        return pltpu.VMEM((2, blocks // 2 * chan, 2 * chan), BF)

    a_mine, a_other = call(
        functools.partial(coarse_grad_body, half), [dealt(56)] * 2, flags, *rows, delta,
        scratch=(halves(56),), smem=1,
    )
    a_keep, a_send = halved(flags, (a_mine, swapped(a_other, 1)))
    a_got = swapped(a_send, 2)
    pg, second = call(
        functools.partial(second_delta_body, half), [coarse, two],
        *delta_rows, coarse_b, down_b, skip, slope2,
    )
    second_rows = [from_before(second), second, from_after(second)]
    a_chunks = chunks(flags, a_keep, tied(a_got, second))
    b_mine, b_other = call(
        second_grad_body, [dealt(22)] * 2, flags, f0, f1, f2, f3, second, act_t, pg,
        scratch=fine_grad_scratch(num, chan, deep) + (halves(22),), smem=1,
    )
    b_got = swapped(b_other, 1)
    a_got = sent(a_chunks[1:])
    e1, e2, c_mine, c_other = call(
        first_delta_body, [fine, fine] + [dealt(14)] * 2,
        flags, *second_rows, second_b, slope1, v0, v1, v2, v3,
        scratch=fine_grad_scratch(num, chan, deep) + (halves(14),), smem=1,
    )
    a_part = summed(tied(a_chunks[0], c_mine), *a_got)
    a_got = sent([a_part] * len(a_got))
    keep, send = halved(flags, (b_mine, b_got), (c_mine, swapped(c_other, 1)))
    got = swapped(send, 2)
    (input_grad,) = call(
        input_grad_body, [((2, chan, num, deep), F32)],
        tied(second_rows[0], keep), *second_rows[1:], second_b, slope1, e1, e2, first_b,
        scratch=(pltpu.VMEM((num, chan, deep), F32), pltpu.VMEM(*fine), pltpu.VMEM(*fine)),
    )
    part = summed(keep, tied(got, input_grad))
    got = sent([part] * (lax.axis_size(AXIS) // 4 - 1))
    a_part = gathered(flags, [tied(a_part, part)] + a_got)
    a_got = swapped(a_part, 2)
    a_pair = paired(flags, a_part, a_got)
    a_got = swapped(a_pair, 1)
    part = summed(part, *got)
    pair = paired(flags, tied(part, a_pair), swapped(part, 2))
    (coarse_out,) = call(
        coarse_unpack, [((27, wide, wide), F32)], flags, tied(a_pair, pair), a_got,
        smem=1, scratch=(halves(56),),
    )
    fine_out = ((27, chan, chan), F32)
    first_out, second_out, down_out = call(
        fine_unpack, [fine_out, fine_out, ((8, chan, wide), F32)], flags, pair, swapped(pair, 1),
        smem=1, scratch=(halves(22), halves(14)),
    )
    return (
        input_grad,
        first_out.reshape(3, 3, 3, chan, chan),
        second_out.reshape(3, 3, 3, chan, chan),
        down_out.reshape(2, 2, 2, chan, wide),
        coarse_out.reshape(3, 3, 3, wide, wide),
    )


def solution(mesh):
    rows = P(("group", "ha"), None, None, None)
    kernels = P("group", None, None, None, None)
    return jax.shard_map(
        body,
        mesh=mesh,
        in_specs=(rows, rows, rows, P(), P(), P(), P()),
        out_specs=(rows, kernels, kernels, kernels, kernels),
        check_vma=False,
    )
```

```python
import functools

import jax
import jax.numpy as jnp
from jax import lax
from jax.experimental import pallas as pl
from jax.experimental.pallas import tpu as pltpu
from jax.sharding import PartitionSpec as P

BF = jnp.bfloat16
F32 = jnp.float32
NT = (((1,), (1,)), ((), ()))
TN = (((0,), (0,)), ((), ()))
AXIS = "ha"
COST = 10**9


def dot(a, b, dims=(((1,), (0,)), ((), ()))):
    return lax.dot_general(a, b, dims, preferred_element_type=F32)


def call(body, outs, *args, scratch=(), smem=0):
    in_specs = [pl.BlockSpec(memory_space=pltpu.SMEM)] * smem
    in_specs += [pl.BlockSpec(memory_space=pltpu.VMEM)] * (len(args) - smem)
    return pl.pallas_call(
        body,
        out_shape=[jax.ShapeDtypeStruct(s, d) for s, d in outs],
        in_specs=in_specs,
        out_specs=[pl.BlockSpec(memory_space=pltpu.VMEM)] * len(outs),
        scratch_shapes=list(scratch),
        compiler_params=pltpu.CompilerParams(vmem_limit_bytes=48 * 2**20),
        cost_estimate=pl.CostEstimate(flops=COST, bytes_accessed=2**20, transcendentals=0),
    )(*args)


def neighbours(array):
    size = lax.axis_size(AXIS)
    up = [(i, i + 1) for i in range(size - 1)]
    down = [(j, i) for i, j in up]
    return up, down


def from_before(array):
    return lax.ppermute(array, AXIS, neighbours(array)[0])


def from_after(array):
    return lax.ppermute(array, AXIS, neighbours(array)[1])


def swapped(array, stride):
    size = lax.axis_size(AXIS)
    return lax.ppermute(array, AXIS, [(i, i ^ stride) for i in range(size)])


def sigmoid(value):
    return 0.5 + 0.5 * jnp.tanh(0.5 * value)


def fine_pair(rows, w_ref, col):
    num = rows[0].shape[0]
    chan, deep = rows[0].shape[1], rows[0].shape[2]
    none = jnp.zeros((chan, deep), BF)
    sides = []
    for at in (col, col + 1):
        tiles = []
        for row in rows:
            for k in (-1, 0, 1):
                tiles.append(row[at + k] if 0 <= at + k < num else none)
        sides.append(jnp.concatenate(tiles, 0))
    y = dot(w_ref[...], jnp.concatenate(sides, 1))
    lane = lax.broadcasted_iota(jnp.int32, (chan, deep), 1)
    outs = []
    for side in range(2):
        part = y[:, side * deep : (side + 1) * deep]
        left = jnp.where(lane == 0, 0.0, pltpu.roll(part[:chan], 1, 1))
        right = jnp.where(lane == deep - 1, 0.0, pltpu.roll(part[2 * chan :], deep - 1, 1))
        outs.append(part[chan : 2 * chan] + left + right)
    return outs


def put(halves, block, value):
    num = value.shape[0]
    each = halves.shape[1] // num
    at = block % each * num
    halves[block // each, at : at + num, :] = value


def deal(halves, bit, mine, other):
    mine[...] = halves[bit]
    other[...] = halves[1 - bit]


def fine_grad(sources, deltas, a_scr, b_scr, halves):
    num, chan, deep = deltas[0].shape
    lane = lax.broadcasted_iota(jnp.int32, (chan, deep), 1)
    for r in range(2):
        for at in range(num):
            cols = slice((r * num + at) * deep, (r * num + at + 1) * deep)
            for kh in range(3):
                for kw in range(3):
                    tap = kh * 3 + kw
                    src = at + kw - 1
                    tile = sources[r + kh][src] if 0 <= src < num else jnp.zeros((chan, deep), BF)
                    a_scr[tap * chan : (tap + 1) * chan, cols] = tile
            value = deltas[r][at]
            wide = value.astype(F32)
            b_scr[:chan, cols] = jnp.where(
                lane == deep - 1, 0.0, pltpu.roll(wide, deep - 1, 1)
            ).astype(BF)
            b_scr[chan : 2 * chan, cols] = value
            b_scr[2 * chan :, cols] = jnp.where(lane == 0, 0.0, pltpu.roll(wide, 1, 1)).astype(BF)
    acc = dot(a_scr[...], b_scr[...], NT).astype(BF)
    for tap in range(9):
        put(halves, tap, acc[tap * chan : (tap + 1) * chan, : 2 * chan])
    for tap in range(0, 10, 2):
        first = acc[tap * chan : (tap + 1) * chan, 2 * chan :]
        if tap + 1 < 9:
            other = acc[(tap + 1) * chan : (tap + 2) * chan, 2 * chan :]
        else:
            other = jnp.zeros_like(first)
        put(halves, 9 + tap // 2, jnp.concatenate([first, other], 1))


def fine_grad_scratch(num, chan, deep):
    return (
        pltpu.VMEM((9 * chan, 2 * num * deep), BF),
        pltpu.VMEM((3 * chan, 2 * num * deep), BF),
    )


def coarse_stack(rows, deep):
    size, chan = rows[0].shape
    none = jnp.zeros((deep, chan), BF)
    tiles = []
    for row in rows:
        value = row[...]
        tiles.append(jnp.concatenate([none, value[: size - deep]], 0))
        tiles.append(value)
        tiles.append(jnp.concatenate([value[deep:], none], 0))
    return jnp.concatenate(tiles, 1)


def coarse_conv(rows, w_ref, deep, *dims):
    size, chan = rows[0].shape
    y = dot(coarse_stack(rows, deep), w_ref[...], *dims)
    at = lax.rem(lax.broadcasted_iota(jnp.int32, (size, chan), 0), deep)
    left = jnp.where(at == 0, 0.0, pltpu.roll(y[:, :chan], 1, 0))
    right = jnp.where(at == deep - 1, 0.0, pltpu.roll(y[:, 2 * chan :], size - 1, 0))
    return y[:, chan : 2 * chan] + left + right


def prepare_kernel(
    volume, skip, w_first, w_second, w_down, w_coarse,
    v0, v1, skip_t, first_f, second_f, first_b, second_b, coarse_f, coarse_b, down_f, down_b,
):
    chan = w_first.shape[1]
    wide = w_coarse.shape[1]
    eye = (
        lax.broadcasted_iota(jnp.int32, (chan, chan), 0)
        == lax.broadcasted_iota(jnp.int32, (chan, chan), 1)
    ).astype(BF)
    for w, ahead, back in ((w_first, first_f, first_b), (w_second, second_f, second_b)):
        for kd in range(3):
            stack = jnp.concatenate([w[3 * j + kd] for j in range(9)], 0)
            ahead[kd * chan : (kd + 1) * chan, :] = dot(eye, stack, NT).astype(BF)
            back[kd * chan : (kd + 1) * chan, :] = jnp.concatenate(
                [w[26 - 3 * j - kd] for j in range(9)], 1
            )
    for j in range(9):
        for kd in range(3):
            rows = slice(j * wide, (j + 1) * wide)
            cols = slice(kd * wide, (kd + 1) * wide)
            coarse_f[rows, cols] = w_coarse[3 * j + kd]
            coarse_b[cols, rows] = w_coarse[26 - 3 * j - kd]
    for a in range(2):
        for b in range(2):
            for c in range(2):
                value = w_down[4 * a + 2 * b + c]
                at = 4 * a + 2 * c + b
                down_f[at * chan : (at + 1) * chan, :] = value
                at = 2 * a + b
                down_b[at * chan : (at + 1) * chan, c * wide : (c + 1) * wide] = value
    for r, out in enumerate((v0, v1)):
        out[...] = pltpu.einshape("cwd->wcd", volume[r])
        skip_t[r] = pltpu.einshape("cwd->wcd", skip[r])


def forward_kernel(
    flags, before, own0, own1, after, w_first, w_second, w_down,
    v0, v3, f0, f1, f2, f3, slope1, slope2, act_t, pooled, rows_scr,
):
    num, chan, deep = own0.shape
    half = deep // 2
    firsts = [f0, f1, f2, f3]
    rows_scr[0] = pltpu.einshape("cwd->wcd", before[0])
    v0[...] = pltpu.einshape("cwd->wcd", before[1])
    v3[...] = pltpu.einshape("cwd->wcd", after[0])
    rows_scr[1] = pltpu.einshape("cwd->wcd", after[1])
    sources = [rows_scr.at[0], v0, own0, own1, v3, rows_scr.at[1]]
    for r in range(4):
        for col in range(0, num, 2):
            for side, pre in enumerate(fine_pair(sources[r : r + 3], w_first, col)):
                sigma = sigmoid(pre)
                act = pre * sigma
                if r == 0:
                    act = jnp.where(flags[0] > 0, act, 0.0)
                if r == 3:
                    act = jnp.where(flags[1] > 0, act, 0.0)
                firsts[r][col + side] = act.astype(BF)
                if 1 <= r <= 2:
                    slope1[r - 1, col + side] = sigma + act * (1.0 - sigma)
    at = lax.broadcasted_iota(jnp.int32, (deep, deep), 1)
    q = lax.broadcasted_iota(jnp.int32, (deep, deep), 0)
    perm = (at == 2 * lax.rem(q, half) + (q >= half).astype(jnp.int32)).astype(BF)
    for r in range(2):
        rows = firsts[r : r + 3]
        for col in range(0, num, 2):
            for side, pre in enumerate(fine_pair(rows, w_second, col)):
                sigma = sigmoid(pre)
                act = pre * sigma
                rows_scr[r, col + side] = act.astype(BF)
                slope2[r, col + side] = sigma + act * (1.0 - sigma)
    wide = 2 * chan
    for r in range(2):
        turned = dot(perm, rows_scr[r].reshape(num * chan, deep), NT).astype(BF)
        for q in range(num // 2):
            for c in range(2):
                lanes = slice((2 * r + c) * wide, (2 * r + c + 1) * wide)
                act_t[q * half : (q + 1) * half, lanes] = turned[
                    c * half : (c + 1) * half, q * wide : (q + 1) * wide
                ]
    pooled[...] = dot(act_t[...], w_down[...]).astype(BF)


def coarse_delta_body(deep, before, own, after, grad, w, delta):
    pre = coarse_conv([before, own, after], w, deep)
    sigma = sigmoid(pre)
    slope = sigma + pre * sigma * (1.0 - sigma)
    delta[...] = (grad[...].astype(F32) * slope).astype(BF)


def coarse_grad_body(deep, flags, before, own, after, delta, mine, other, halves):
    size, chan = own.shape
    wide = delta[...].astype(F32)
    at = lax.rem(lax.broadcasted_iota(jnp.int32, (size, chan), 0), deep)
    up = jnp.where(at == deep - 1, 0.0, pltpu.roll(wide, size - 1, 0)).astype(BF)
    down = jnp.where(at == 0, 0.0, pltpu.roll(wide, 1, 0)).astype(BF)
    moved = jnp.concatenate([up, delta[...], down], 1)
    stack = coarse_stack([before, own, after], deep)
    acc = dot(stack, moved, TN).astype(BF)
    piece = chan // 2
    for k in range(3):
        for j in range(18):
            value = acc[j * piece : (j + 1) * piece, k * chan : (k + 1) * chan]
            put(halves, 18 * k + j, value)
    deal(halves, flags[2], mine, other)


def second_delta_body(deep, before, own, after, w, w_up, skip, slope, pg, d0, d1):
    value = coarse_conv([before, own, after], w, deep, NT).astype(BF)
    pg[...] = value
    turned = value.T
    outs = [d0, d1]
    half = d0.shape[1]
    fine = d0.shape[2]
    row = lax.broadcasted_iota(jnp.int32, (fine, 4 * fine), 0)
    lane = lax.broadcasted_iota(jnp.int32, (fine, 4 * fine), 1)
    odd = (lax.rem(lane, 2 * fine) >= fine).astype(jnp.int32)
    same = (lane >= 2 * fine) == (row >= deep)
    spread = (same & (lax.rem(lane, fine) == 2 * lax.rem(row, deep) + odd)).astype(BF)
    for m in range(turned.shape[1] // (2 * deep)):
        up = dot(turned[:, 2 * m * deep : 2 * (m + 1) * deep], spread).astype(BF)
        parts = [
            jnp.concatenate([up[:, (2 * s + c) * fine : (2 * s + c + 1) * fine] for s in range(2)], 1)
            for c in range(2)
        ]
        back = dot(w_up[...], jnp.concatenate(parts, 0))
        for s in range(2):
            for a in range(2):
                for b in range(2):
                    rows = slice((2 * a + b) * half, (2 * a + b + 1) * half)
                    at = 4 * m + 2 * s + b
                    total = back[rows, s * fine : (s + 1) * fine] + skip[a, at].astype(F32)
                    outs[a][at] = (total * slope[a, at]).astype(BF)


def second_grad_body(flags, s0, s1, s2, s3, d0, d1, act_t, pg, mine, other, a_scr, b_scr, halves):
    fine_grad([s0, s1, s2, s3], [d0, d1], a_scr, b_scr, halves)
    down = dot(act_t[...], pg[...], TN).astype(BF)
    chan = s0.shape[1]
    for j in range(8):
        put(halves, 14 + j, down[j * chan : (j + 1) * chan])
    deal(halves, flags[2], mine, other)


def back_row(rows, w, slope, at, out):
    for col in range(0, out.shape[0], 2):
        for side, value in enumerate(fine_pair(rows, w, col)):
            out[col + side] = (value * slope[at, col + side]).astype(BF)


def first_delta_body(
    flags, before, d0, d1, after, w, slope, s0, s1, s2, s3, e1, e2, mine, other, a_scr, b_scr, halves
):
    rows = [before, d0, d1, after]
    back_row(rows[:3], w, slope, 0, e1)
    back_row(rows[1:], w, slope, 1, e2)
    fine_grad([s0, s1, s2, s3], [e1, e2], a_scr, b_scr, halves)
    deal(halves, flags[2], mine, other)


def input_grad_body(before, e1, e2, after, w, out, scr):
    rows = [before, e1, e2, after]
    for r in range(2):
        for col in range(0, e1.shape[0], 2):
            for side, value in enumerate(fine_pair(rows[r : r + 3], w, col)):
                scr[col + side] = value
        out[r] = pltpu.einshape("wcd->cwd", scr[...])


def split_body(count, flags, *refs):
    keep, send = refs[2 * count :]
    at = 0
    for mine, got in zip(refs[:count], refs[count : 2 * count]):
        half = mine.shape[0] // 2
        for side in range(2):
            rows = slice(side * half, (side + 1) * half)
            total = (mine[rows, :].astype(F32) + got[rows, :].astype(F32)).astype(BF)

            @pl.when(flags[3] == side)
            def _():
                keep[at : at + half, :] = total

            @pl.when(flags[3] != side)
            def _():
                send[at : at + half, :] = total

        at += half


def add_body(mine, got, out):
    out[...] = (mine[...].astype(F32) + got[...].astype(F32)).astype(BF)


def order_body(flags, mine, got, out):
    bit = flags[3]
    out[bit] = mine[...].reshape(out.shape[1:])
    out[1 - bit] = got[...].reshape(out.shape[1:])


def block_of(halves, block, num):
    each = halves.shape[1] // num
    at = block % each * num
    return halves[block // each, at : at + num, :].astype(F32)


def fine_blocks(halves, out):
    chan = out.shape[1]
    for tap in range(9):
        value = block_of(halves, tap, chan)
        out[3 * tap] = value[:, :chan]
        out[3 * tap + 1] = value[:, chan:]
        value = block_of(halves, 9 + tap // 2, chan)
        out[3 * tap + 2] = value[:, chan:] if tap % 2 else value[:, :chan]


def gather_halves(flags, mine, got, *arrays):
    at = 0
    for halves in arrays:
        rows = halves.shape[1] // 2
        for side in range(2):
            to = slice(side * rows, (side + 1) * rows)
            halves[flags[2], to, :] = mine[side, at : at + rows, :]
            halves[1 - flags[2], to, :] = got[side, at : at + rows, :]
        at += rows


def fine_unpack(flags, mine, got, first, second, down, middle_halves, first_halves):
    gather_halves(flags, mine, got, middle_halves, first_halves)
    fine_blocks(first_halves, first)
    fine_blocks(middle_halves, second)
    chan = first.shape[1]
    for a in range(2):
        for b in range(2):
            for c in range(2):
                down[4 * a + 2 * b + c] = block_of(middle_halves, 14 + 4 * a + 2 * c + b, chan)


def coarse_unpack(flags, mine, got, out, halves):
    gather_halves(flags, mine, got, halves)
    piece = out.shape[1] // 2
    for k in range(3):
        for j in range(9):
            for s in range(2):
                out[3 * j + k, s * piece : (s + 1) * piece, :] = block_of(
                    halves, 18 * k + 2 * j + s, piece
                )


def tied(first, *others):
    return lax.optimization_barrier((first,) + others)[0]


def halved(flags, *pairs):
    mine, got = zip(*pairs)
    rows = sum(m.shape[0] for m in mine) // 2
    return call(
        functools.partial(split_body, len(pairs)), [((rows, mine[0].shape[1]), BF)] * 2,
        flags, *mine, *got, smem=1,
    )


def summed(mine, got):
    return call(add_body, [(mine.shape, BF)], mine, got)[0]


def paired(flags, part, got):
    lanes = part.shape[-1]
    return call(
        order_body, [((2, part.size // lanes, lanes), BF)], flags, part, got, smem=1
    )[0]


def body(volume, skip_grad, coarse_grad, w_first, w_second, w_down, w_coarse):
    _, chan, num, deep = volume.shape
    wide = w_coarse.shape[-1]
    half = deep // 2
    size = num // 2 * half
    index = lax.axis_index(AXIS)
    flags = jnp.stack(
        [index, lax.axis_size(AXIS) - 1 - index, index % 2, (index // 2) % 2]
    ).astype(jnp.int32)

    fine = ((num, chan, deep), BF)
    coarse = ((size, wide), BF)
    two = ((2, num, chan, deep), BF)

    before, after = from_before(volume), from_after(volume)
    v1, v2, skip, first_f, second_f, first_b, second_b, coarse_f, coarse_b, down_f, down_b = call(
        prepare_kernel,
        [fine, fine, two]
        + [((3 * chan, 9 * chan), BF)] * 4
        + [((9 * wide, 3 * wide), BF), ((3 * wide, 9 * wide), BF)]
        + [((8 * chan, wide), BF), ((4 * chan, 2 * wide), BF)],
        volume, skip_grad,
        w_first.reshape(27, chan, chan), w_second.reshape(27, chan, chan),
        w_down.reshape(8, chan, wide), w_coarse.reshape(27, wide, wide),
    )
    v0, v3, f0, f1, f2, f3, slope1, slope2, act_t, pooled = call(
        forward_kernel,
        [fine] * 6 + [(two[0], F32)] * 2 + [((size, 8 * chan), BF), coarse],
        flags, before, v1, v2, after, first_f, second_f, down_f,
        scratch=(pltpu.VMEM(*two),),
        smem=1,
    )
    rows = [from_before(pooled), pooled, from_after(pooled)]
    (delta,) = call(
        functools.partial(coarse_delta_body, half), [coarse],
        *rows, coarse_grad.reshape(size, wide), coarse_f,
    )
    delta_rows = [from_before(delta), delta, from_after(delta)]

    def dealt(blocks):
        return ((blocks // 2 * chan, 2 * chan), BF)

    def halves(blocks):
        return pltpu.VMEM((2, blocks // 2 * chan, 2 * chan), BF)

    a_mine, a_other = call(
        functools.partial(coarse_grad_body, half), [dealt(54)] * 2, flags, *rows, delta,
        scratch=(halves(54),), smem=1,
    )
    pg, d0, d1 = call(
        functools.partial(second_delta_body, half), [coarse, fine, fine],
        *delta_rows, coarse_b, down_b, skip, slope2,
    )
    second_rows = [from_before(d1), d0, d1, from_after(d0)]
    b_mine, b_other = call(
        second_grad_body, [dealt(22)] * 2, flags, f0, f1, f2, f3, d0, d1, act_t, pg,
        scratch=fine_grad_scratch(num, chan, deep) + (halves(22),), smem=1,
    )
    a_keep, a_send = halved(flags, (a_mine, tied(swapped(a_other, 1), b_mine)))
    b_got = swapped(b_other, 1)
    e1, e2, c_mine, c_other = call(
        first_delta_body, [fine, fine] + [dealt(14)] * 2,
        flags, *second_rows, second_b, slope1, v0, v1, v2, v3,
        scratch=fine_grad_scratch(num, chan, deep) + (halves(14),), smem=1,
    )
    a_got = swapped(tied(a_send, c_mine), 2)
    keep, send = halved(flags, (b_mine, b_got), (c_mine, swapped(c_other, 1)))
    got = swapped(send, 2)
    first_rows = [from_before(tied(e2, keep)), e1, e2, from_after(tied(e1, keep))]
    a_part, part = summed(a_keep, tied(a_got, keep)), None
    strides = []
    stride = 4
    while stride < lax.axis_size(AXIS):
        strides.append(stride)
        stride *= 2
    for stride in strides:
        a_got = swapped(a_part, stride)
        part = summed(keep, tied(got, a_part)) if part is None else summed(part, tied(got, a_part))
        got = swapped(part, stride)
        a_part = summed(a_part, tied(a_got, part))
    a_got = swapped(a_part, 2)
    (input_grad,) = call(
        input_grad_body, [((2, chan, num, deep), F32)],
        tied(first_rows[0], a_part), *first_rows[1:], first_b,
        scratch=(pltpu.VMEM((num, chan, deep), F32),),
    )
    part = summed(part, tied(got, a_part, input_grad))
    got = swapped(part, 2)
    a_pair = paired(flags, tied(a_part, part), a_got)
    a_got = swapped(a_pair, 1)
    pair = paired(flags, tied(part, a_pair), got)
    (coarse_out,) = call(
        coarse_unpack, [((27, wide, wide), F32)], flags, tied(a_pair, pair), a_got,
        smem=1, scratch=(halves(54),),
    )
    fine_out = ((27, chan, chan), F32)
    first_out, second_out, down_out = call(
        fine_unpack, [fine_out, fine_out, ((8, chan, wide), F32)],
        flags, tied(pair, coarse_out), swapped(pair, 1),
        smem=1, scratch=(halves(22), halves(14)),
    )
    return (
        input_grad,
        first_out.reshape(3, 3, 3, chan, chan),
        second_out.reshape(3, 3, 3, chan, chan),
        down_out.reshape(2, 2, 2, chan, wide),
        coarse_out.reshape(3, 3, 3, wide, wide),
    )


def solution(mesh):
    rows = P(("group", "ha"), None, None, None)
    kernels = P("group", None, None, None, None)
    return jax.shard_map(
        body,
        mesh=mesh,
        in_specs=(rows, rows, rows, P(), P(), P(), P()),
        out_specs=(rows, kernels, kernels, kernels, kernels),
        check_vma=False,
    )
```

```python
import functools

import jax
import jax.numpy as jnp
from jax import lax
from jax.experimental import pallas as pl
from jax.experimental.pallas import tpu as pltpu
from jax.sharding import PartitionSpec as P

BF = jnp.bfloat16
F32 = jnp.float32
NT = (((1,), (1,)), ((), ()))
TN = (((0,), (0,)), ((), ()))
AXIS = "ha"
COST = 4 * 10**9


def dot(a, b, dims=(((1,), (0,)), ((), ()))):
    return lax.dot_general(a, b, dims, preferred_element_type=F32)


def call(body, outs, *args, scratch=(), smem=0):
    in_specs = [pl.BlockSpec(memory_space=pltpu.SMEM)] * smem
    in_specs += [pl.BlockSpec(memory_space=pltpu.VMEM)] * (len(args) - smem)
    return pl.pallas_call(
        body,
        out_shape=[jax.ShapeDtypeStruct(s, d) for s, d in outs],
        in_specs=in_specs,
        out_specs=[pl.BlockSpec(memory_space=pltpu.VMEM)] * len(outs),
        scratch_shapes=list(scratch),
        compiler_params=pltpu.CompilerParams(vmem_limit_bytes=48 * 2**20),
        cost_estimate=pl.CostEstimate(flops=COST, bytes_accessed=2**20, transcendentals=0),
    )(*args)


def neighbours(array):
    size = lax.axis_size(AXIS)
    up = [(i, i + 1) for i in range(size - 1)]
    down = [(j, i) for i, j in up]
    return up, down


def from_before(array):
    return lax.ppermute(array, AXIS, neighbours(array)[0])


def from_after(array):
    return lax.ppermute(array, AXIS, neighbours(array)[1])


def swapped(array, stride):
    size = lax.axis_size(AXIS)
    return lax.ppermute(array, AXIS, [(i, i ^ stride) for i in range(size)])


def sigmoid(value):
    return 0.5 + 0.5 * jnp.tanh(0.5 * value)


def fine_pair(rows, w_ref, col):
    num = rows[0].shape[0]
    chan, deep = rows[0].shape[1], rows[0].shape[2]
    none = jnp.zeros((chan, deep), BF)
    sides = []
    for at in (col, col + 1):
        tiles = []
        for row in rows:
            for k in (-1, 0, 1):
                tiles.append(row[at + k] if 0 <= at + k < num else none)
        sides.append(jnp.concatenate(tiles, 0))
    y = dot(w_ref[...], jnp.concatenate(sides, 1))
    lane = lax.broadcasted_iota(jnp.int32, (chan, deep), 1)
    outs = []
    for side in range(2):
        part = y[:, side * deep : (side + 1) * deep]
        left = jnp.where(lane == 0, 0.0, pltpu.roll(part[:chan], 1, 1))
        right = jnp.where(lane == deep - 1, 0.0, pltpu.roll(part[2 * chan :], deep - 1, 1))
        outs.append(part[chan : 2 * chan] + left + right)
    return outs


def put(halves, block, value):
    num = value.shape[0]
    each = halves.shape[1] // num
    at = block % each * num
    halves[block // each, at : at + num, :] = value


def deal(halves, bit, mine, other):
    mine[...] = halves[bit]
    other[...] = halves[1 - bit]


def fine_grad(sources, deltas, a_scr, b_scr, halves):
    num, chan, deep = deltas[0].shape
    lane = lax.broadcasted_iota(jnp.int32, (chan, deep), 1)
    for r in range(2):
        for at in range(num):
            cols = slice((r * num + at) * deep, (r * num + at + 1) * deep)
            for kh in range(3):
                for kw in range(3):
                    tap = kh * 3 + kw
                    src = at + kw - 1
                    tile = sources[r + kh][src] if 0 <= src < num else jnp.zeros((chan, deep), BF)
                    a_scr[tap * chan : (tap + 1) * chan, cols] = tile
            value = deltas[r][at]
            wide = value.astype(F32)
            b_scr[:chan, cols] = jnp.where(
                lane == deep - 1, 0.0, pltpu.roll(wide, deep - 1, 1)
            ).astype(BF)
            b_scr[chan : 2 * chan, cols] = value
            b_scr[2 * chan :, cols] = jnp.where(lane == 0, 0.0, pltpu.roll(wide, 1, 1)).astype(BF)
    acc = dot(a_scr[...], b_scr[...], NT).astype(BF)
    for tap in range(9):
        put(halves, tap, acc[tap * chan : (tap + 1) * chan, : 2 * chan])
    for tap in range(0, 10, 2):
        first = acc[tap * chan : (tap + 1) * chan, 2 * chan :]
        if tap + 1 < 9:
            other = acc[(tap + 1) * chan : (tap + 2) * chan, 2 * chan :]
        else:
            other = jnp.zeros_like(first)
        put(halves, 9 + tap // 2, jnp.concatenate([first, other], 1))


def fine_grad_scratch(num, chan, deep):
    return (
        pltpu.VMEM((9 * chan, 2 * num * deep), BF),
        pltpu.VMEM((3 * chan, 2 * num * deep), BF),
    )


def coarse_stack(rows, deep):
    size, chan = rows[0].shape
    none = jnp.zeros((deep, chan), BF)
    tiles = []
    for row in rows:
        value = row[...]
        tiles.append(jnp.concatenate([none, value[: size - deep]], 0))
        tiles.append(value)
        tiles.append(jnp.concatenate([value[deep:], none], 0))
    return jnp.concatenate(tiles, 1)


def coarse_conv(rows, w_ref, deep, *dims):
    size, chan = rows[0].shape
    y = dot(coarse_stack(rows, deep), w_ref[...], *dims)
    at = lax.rem(lax.broadcasted_iota(jnp.int32, (size, chan), 0), deep)
    left = jnp.where(at == 0, 0.0, pltpu.roll(y[:, :chan], 1, 0))
    right = jnp.where(at == deep - 1, 0.0, pltpu.roll(y[:, 2 * chan :], size - 1, 0))
    return y[:, chan : 2 * chan] + left + right


def prepare_kernel(
    volume, skip, w_first, w_second, w_down, w_coarse,
    v0, v1, skip_t, first_f, second_f, first_b, second_b, coarse_f, coarse_b, down_f, down_b,
):
    chan = w_first.shape[1]
    wide = w_coarse.shape[1]
    eye = (
        lax.broadcasted_iota(jnp.int32, (chan, chan), 0)
        == lax.broadcasted_iota(jnp.int32, (chan, chan), 1)
    ).astype(BF)
    for w, ahead, back in ((w_first, first_f, first_b), (w_second, second_f, second_b)):
        for kd in range(3):
            stack = jnp.concatenate([w[3 * j + kd] for j in range(9)], 0)
            ahead[kd * chan : (kd + 1) * chan, :] = dot(eye, stack, NT).astype(BF)
            back[kd * chan : (kd + 1) * chan, :] = jnp.concatenate(
                [w[26 - 3 * j - kd] for j in range(9)], 1
            )
    for j in range(9):
        for kd in range(3):
            rows = slice(j * wide, (j + 1) * wide)
            cols = slice(kd * wide, (kd + 1) * wide)
            coarse_f[rows, cols] = w_coarse[3 * j + kd]
            coarse_b[cols, rows] = w_coarse[26 - 3 * j - kd]
    for a in range(2):
        for b in range(2):
            for c in range(2):
                value = w_down[4 * a + 2 * b + c]
                at = 4 * a + 2 * c + b
                down_f[at * chan : (at + 1) * chan, :] = value
                at = 2 * a + b
                down_b[at * chan : (at + 1) * chan, c * wide : (c + 1) * wide] = value
    for r, out in enumerate((v0, v1)):
        out[...] = pltpu.einshape("cwd->wcd", volume[r])
        skip_t[r] = pltpu.einshape("cwd->wcd", skip[r])


def forward_kernel(
    flags, before, own0, own1, after, w_first, w_second, w_down,
    v0, v3, f0, f1, f2, f3, slope1, slope2, act_t, pooled, rows_scr,
):
    num, chan, deep = own0.shape
    half = deep // 2
    firsts = [f0, f1, f2, f3]
    rows_scr[0] = pltpu.einshape("cwd->wcd", before[0])
    v0[...] = pltpu.einshape("cwd->wcd", before[1])
    v3[...] = pltpu.einshape("cwd->wcd", after[0])
    rows_scr[1] = pltpu.einshape("cwd->wcd", after[1])
    sources = [rows_scr.at[0], v0, own0, own1, v3, rows_scr.at[1]]
    for r in range(4):
        for col in range(0, num, 2):
            for side, pre in enumerate(fine_pair(sources[r : r + 3], w_first, col)):
                sigma = sigmoid(pre)
                act = pre * sigma
                if r == 0:
                    act = jnp.where(flags[0] > 0, act, 0.0)
                if r == 3:
                    act = jnp.where(flags[1] > 0, act, 0.0)
                firsts[r][col + side] = act.astype(BF)
                if 1 <= r <= 2:
                    slope1[r - 1, col + side] = sigma + act * (1.0 - sigma)
    at = lax.broadcasted_iota(jnp.int32, (deep, deep), 1)
    q = lax.broadcasted_iota(jnp.int32, (deep, deep), 0)
    perm = (at == 2 * lax.rem(q, half) + (q >= half).astype(jnp.int32)).astype(BF)
    for r in range(2):
        rows = firsts[r : r + 3]
        for col in range(0, num, 2):
            for side, pre in enumerate(fine_pair(rows, w_second, col)):
                sigma = sigmoid(pre)
                act = pre * sigma
                rows_scr[r, col + side] = act.astype(BF)
                slope2[r, col + side] = sigma + act * (1.0 - sigma)
    wide = 2 * chan
    for r in range(2):
        turned = dot(perm, rows_scr[r].reshape(num * chan, deep), NT).astype(BF)
        for q in range(num // 2):
            for c in range(2):
                lanes = slice((2 * r + c) * wide, (2 * r + c + 1) * wide)
                act_t[q * half : (q + 1) * half, lanes] = turned[
                    c * half : (c + 1) * half, q * wide : (q + 1) * wide
                ]
    pooled[...] = dot(act_t[...], w_down[...]).astype(BF)


def coarse_delta_body(deep, before, own, after, grad, w, delta):
    pre = coarse_conv([before, own, after], w, deep)
    sigma = sigmoid(pre)
    slope = sigma + pre * sigma * (1.0 - sigma)
    delta[...] = (grad[...].astype(F32) * slope).astype(BF)


def coarse_grad_body(deep, flags, before, own, after, delta, mine, other, halves):
    size, chan = own.shape
    wide = delta[...].astype(F32)
    at = lax.rem(lax.broadcasted_iota(jnp.int32, (size, chan), 0), deep)
    up = jnp.where(at == deep - 1, 0.0, pltpu.roll(wide, size - 1, 0)).astype(BF)
    down = jnp.where(at == 0, 0.0, pltpu.roll(wide, 1, 0)).astype(BF)
    moved = jnp.concatenate([up, delta[...], down], 1)
    stack = coarse_stack([before, own, after], deep)
    acc = dot(stack, moved, TN).astype(BF)
    piece = chan // 2
    for k in range(3):
        for j in range(18):
            value = acc[j * piece : (j + 1) * piece, k * chan : (k + 1) * chan]
            put(halves, 18 * k + j, value)
    deal(halves, flags[2], mine, other)


def second_delta_body(deep, before, own, after, w, w_up, skip, slope, pg, d0, d1):
    value = coarse_conv([before, own, after], w, deep, NT).astype(BF)
    pg[...] = value
    turned = value.T
    outs = [d0, d1]
    half = d0.shape[1]
    fine = d0.shape[2]
    row = lax.broadcasted_iota(jnp.int32, (fine, 4 * fine), 0)
    lane = lax.broadcasted_iota(jnp.int32, (fine, 4 * fine), 1)
    odd = (lax.rem(lane, 2 * fine) >= fine).astype(jnp.int32)
    same = (lane >= 2 * fine) == (row >= deep)
    spread = (same & (lax.rem(lane, fine) == 2 * lax.rem(row, deep) + odd)).astype(BF)
    for m in range(turned.shape[1] // (2 * deep)):
        up = dot(turned[:, 2 * m * deep : 2 * (m + 1) * deep], spread).astype(BF)
        parts = [
            jnp.concatenate([up[:, (2 * s + c) * fine : (2 * s + c + 1) * fine] for s in range(2)], 1)
            for c in range(2)
        ]
        back = dot(w_up[...], jnp.concatenate(parts, 0))
        for s in range(2):
            for a in range(2):
                for b in range(2):
                    rows = slice((2 * a + b) * half, (2 * a + b + 1) * half)
                    at = 4 * m + 2 * s + b
                    total = back[rows, s * fine : (s + 1) * fine] + skip[a, at].astype(F32)
                    outs[a][at] = (total * slope[a, at]).astype(BF)


def second_grad_body(flags, s0, s1, s2, s3, d0, d1, act_t, pg, mine, other, a_scr, b_scr, halves):
    fine_grad([s0, s1, s2, s3], [d0, d1], a_scr, b_scr, halves)
    down = dot(act_t[...], pg[...], TN).astype(BF)
    chan = s0.shape[1]
    for j in range(8):
        put(halves, 14 + j, down[j * chan : (j + 1) * chan])
    deal(halves, flags[2], mine, other)


def back_row(rows, w, slope, at, out):
    for col in range(0, out.shape[0], 2):
        for side, value in enumerate(fine_pair(rows, w, col)):
            out[col + side] = (value * slope[at, col + side]).astype(BF)


def first_delta_body(
    flags, before, d0, d1, after, w, slope, s0, s1, s2, s3, e1, e2, mine, other, a_scr, b_scr, halves
):
    rows = [before, d0, d1, after]
    back_row(rows[:3], w, slope, 0, e1)
    back_row(rows[1:], w, slope, 1, e2)
    fine_grad([s0, s1, s2, s3], [e1, e2], a_scr, b_scr, halves)
    deal(halves, flags[2], mine, other)


def input_grad_body(before, e1, e2, after, w, out, scr):
    rows = [before, e1, e2, after]
    for r in range(2):
        for col in range(0, e1.shape[0], 2):
            for side, value in enumerate(fine_pair(rows[r : r + 3], w, col)):
                scr[col + side] = value
        out[r] = pltpu.einshape("wcd->cwd", scr[...])


def split_body(count, flags, *refs):
    keep, send = refs[2 * count :]
    at = 0
    for mine, got in zip(refs[:count], refs[count : 2 * count]):
        half = mine.shape[0] // 2
        for side in range(2):
            rows = slice(side * half, (side + 1) * half)
            total = (mine[rows, :].astype(F32) + got[rows, :].astype(F32)).astype(BF)

            @pl.when(flags[3] == side)
            def _():
                keep[at : at + half, :] = total

            @pl.when(flags[3] != side)
            def _():
                send[at : at + half, :] = total

        at += half


def add_body(mine, got, out):
    out[...] = (mine[...].astype(F32) + got[...].astype(F32)).astype(BF)


def order_body(count, flags, *refs):
    bit = flags[3]
    out = refs[-1]
    at = 0
    for mine, got in zip(refs[:count], refs[count : 2 * count]):
        rows = slice(at, at + mine.shape[0])
        out[bit, rows, :] = mine[...]
        out[1 - bit, rows, :] = got[...]
        at += mine.shape[0]


def block_of(halves, block, num):
    each = halves.shape[1] // num
    at = block % each * num
    return halves[block // each, at : at + num, :].astype(F32)


def fine_blocks(halves, out):
    chan = out.shape[1]
    for tap in range(9):
        value = block_of(halves, tap, chan)
        out[3 * tap] = value[:, :chan]
        out[3 * tap + 1] = value[:, chan:]
        value = block_of(halves, 9 + tap // 2, chan)
        out[3 * tap + 2] = value[:, chan:] if tap % 2 else value[:, :chan]


def gather_halves(flags, mine, got, *arrays):
    at = 0
    for halves in arrays:
        rows = halves.shape[1] // 2
        for side in range(2):
            to = slice(side * rows, (side + 1) * rows)
            halves[flags[2], to, :] = mine[side, at : at + rows, :]
            halves[1 - flags[2], to, :] = got[side, at : at + rows, :]
        at += rows


def unpack_body(
    flags, mine, got, first, second, down, coarse, coarse_halves, middle_halves, first_halves
):
    gather_halves(flags, mine, got, coarse_halves, middle_halves, first_halves)
    fine_blocks(first_halves, first)
    fine_blocks(middle_halves, second)
    chan = first.shape[1]
    for a in range(2):
        for b in range(2):
            for c in range(2):
                down[4 * a + 2 * b + c] = block_of(middle_halves, 14 + 4 * a + 2 * c + b, chan)
    piece = coarse.shape[1] // 2
    for k in range(3):
        for j in range(9):
            for s in range(2):
                coarse[3 * j + k, s * piece : (s + 1) * piece, :] = block_of(
                    coarse_halves, 18 * k + 2 * j + s, piece
                )


def tied(first, *others):
    return lax.optimization_barrier((first,) + others)[0]


def halved(flags, *pairs):
    mine, got = zip(*pairs)
    rows = sum(m.shape[0] for m in mine) // 2
    return call(
        functools.partial(split_body, len(pairs)), [((rows, mine[0].shape[1]), BF)] * 2,
        flags, *mine, *got, smem=1,
    )


def summed(mine, got):
    return call(add_body, [(mine.shape, BF)], mine, got)[0]


def paired(flags, *pairs):
    mine, got = zip(*pairs)
    rows = sum(m.shape[0] for m in mine)
    return call(
        functools.partial(order_body, len(pairs)), [((2, rows, mine[0].shape[1]), BF)],
        flags, *mine, *got, smem=1,
    )[0]


def body(volume, skip_grad, coarse_grad, w_first, w_second, w_down, w_coarse):
    _, chan, num, deep = volume.shape
    wide = w_coarse.shape[-1]
    half = deep // 2
    size = num // 2 * half
    index = lax.axis_index(AXIS)
    flags = jnp.stack(
        [index, lax.axis_size(AXIS) - 1 - index, index % 2, (index // 2) % 2]
    ).astype(jnp.int32)

    fine = ((num, chan, deep), BF)
    coarse = ((size, wide), BF)
    two = ((2, num, chan, deep), BF)

    before, after = from_before(volume), from_after(volume)
    v1, v2, skip, first_f, second_f, first_b, second_b, coarse_f, coarse_b, down_f, down_b = call(
        prepare_kernel,
        [fine, fine, two]
        + [((3 * chan, 9 * chan), BF)] * 4
        + [((9 * wide, 3 * wide), BF), ((3 * wide, 9 * wide), BF)]
        + [((8 * chan, wide), BF), ((4 * chan, 2 * wide), BF)],
        volume, skip_grad,
        w_first.reshape(27, chan, chan), w_second.reshape(27, chan, chan),
        w_down.reshape(8, chan, wide), w_coarse.reshape(27, wide, wide),
    )
    v0, v3, f0, f1, f2, f3, slope1, slope2, act_t, pooled = call(
        forward_kernel,
        [fine] * 6 + [(two[0], F32)] * 2 + [((size, 8 * chan), BF), coarse],
        flags, before, v1, v2, after, first_f, second_f, down_f,
        scratch=(pltpu.VMEM(*two),),
        smem=1,
    )
    rows = [from_before(pooled), pooled, from_after(pooled)]
    (delta,) = call(
        functools.partial(coarse_delta_body, half), [coarse],
        *rows, coarse_grad.reshape(size, wide), coarse_f,
    )
    delta_rows = [from_before(delta), delta, from_after(delta)]

    def dealt(blocks):
        return ((blocks // 2 * chan, 2 * chan), BF)

    def halves(blocks):
        return pltpu.VMEM((2, blocks // 2 * chan, 2 * chan), BF)

    a_mine, a_other = call(
        functools.partial(coarse_grad_body, half), [dealt(54)] * 2, flags, *rows, delta,
        scratch=(halves(54),), smem=1,
    )
    pg, d0, d1 = call(
        functools.partial(second_delta_body, half), [coarse, fine, fine],
        *delta_rows, coarse_b, down_b, skip, slope2,
    )
    second_rows = [from_before(d1), d0, d1, from_after(d0)]
    b_mine, b_other = call(
        second_grad_body, [dealt(22)] * 2, flags, f0, f1, f2, f3, d0, d1, act_t, pg,
        scratch=fine_grad_scratch(num, chan, deep) + (halves(22),), smem=1,
    )
    a_keep, a_send = halved(flags, (a_mine, tied(swapped(a_other, 1), b_mine)))
    a_got = swapped(a_send, 2)
    b_got = swapped(b_other, 1)
    e1, e2, c_mine, c_other = call(
        first_delta_body, [fine, fine] + [dealt(14)] * 2,
        flags, tied(second_rows[0], a_keep), *second_rows[1:], second_b, slope1, v0, v1, v2, v3,
        scratch=fine_grad_scratch(num, chan, deep) + (halves(14),), smem=1,
    )
    a_part = summed(a_keep, tied(a_got, c_mine))
    c_got = swapped(c_other, 1)
    keep, send = halved(flags, (b_mine, tied(b_got, a_part)), (c_mine, c_got))
    got = swapped(send, 2)
    strides = []
    stride = 4
    while stride < lax.axis_size(AXIS):
        strides.append(stride)
        stride *= 2
    a_got = swapped(a_part, strides[0])
    a_part = summed(a_part, tied(a_got, keep))
    a_got = swapped(a_part, strides[1])
    part = summed(keep, tied(got, a_part))
    got = swapped(part, strides[0])
    face = part
    part = summed(part, tied(got, face))
    got = swapped(part, strides[1])
    first_rows = [from_before(tied(e2, face)), e1, e2, from_after(tied(e1, face))]
    for stride in strides[2:]:
        a_part = summed(a_part, tied(a_got, part))
        a_got = swapped(a_part, stride)
        part = summed(part, tied(got, a_part))
        got = swapped(part, stride)
    a_part = summed(a_part, tied(a_got, part))
    a_got = swapped(a_part, 2)
    (input_grad,) = call(
        input_grad_body, [((2, chan, num, deep), F32)],
        tied(first_rows[0], a_part), *first_rows[1:], first_b,
        scratch=(pltpu.VMEM((num, chan, deep), F32),),
    )
    part = summed(part, tied(got, input_grad))
    pair = paired(flags, (a_part, tied(a_got, part)), (part, swapped(part, 2)))
    fine_out = ((27, chan, chan), F32)
    first_out, second_out, down_out, coarse_out = call(
        unpack_body,
        [fine_out, fine_out, ((8, chan, wide), F32), ((27, wide, wide), F32)],
        flags, pair, swapped(pair, 1),
        smem=1, scratch=(halves(54), halves(22), halves(14)),
    )
    return (
        input_grad,
        first_out.reshape(3, 3, 3, chan, chan),
        second_out.reshape(3, 3, 3, chan, chan),
        down_out.reshape(2, 2, 2, chan, wide),
        coarse_out.reshape(3, 3, 3, wide, wide),
    )


def solution(mesh):
    rows = P(("group", "ha"), None, None, None)
    kernels = P("group", None, None, None, None)
    return jax.shard_map(
        body,
        mesh=mesh,
        in_specs=(rows, rows, rows, P(), P(), P(), P()),
        out_specs=(rows, kernels, kernels, kernels, kernels),
        check_vma=False,
    )
```
